256 devices in a mesh: morton: 256 (over y, z, x, core).
Axes of the slice: x: 4, y: 4, z: 8, core: 2. Of those that a mesh axis runs over, the one named last changes fastest.
Arguments:
- offsets: float32 [3, 2097152], P(None, 'morton'), may hold values from -0.5 to 0.5
- forces: float32 [3, 2097152], P(None, 'morton'), may hold values from -6 to 6
- counts: int32 [16384], P('morton'), may hold values from 1 to 128
- uc2ue: float32 [456, 456], replicated, may hold values from -0.25 to 0.25
- m2m_ops: float32 [8, 456, 456], replicated, may hold values from -0.09375 to 0.09375
- compress: float32 [456, 64], replicated, may hold values from -0.25 to 0.25
- m2l_ops: bfloat16 [316, 64, 64], replicated, may hold values from -0.0546875 to 0.0546875
- root_ops: bfloat16 [63, 64, 64], replicated, may hold values from -0.125 to 0.125
Outputs:
- local_boxes: float32 [18688, 64], P('morton')
- local_roots: float32 [32, 64], replicated
The draws below stay inside these ranges and needn't reach their ends.
Inputs may be any that keep to these rules, and one draw needn't show every extreme that they name: The live points of a leaf are its first counts slots; later slots belong to no point.
All inputs are finite; a program needn't handle non-finite values.
Results may differ from the reference program's by a relative error of at most 0.0031.
Values may be sent and summed in bfloat16 or wider, within the bound.
No kernel may reach another device: no remote copies, remote signals or barrier semaphores. Data moves between devices by JAX's collectives and lax.ppermute only.
A program may use at most 192 MiB of HBM per device.

```python
import jax
import jax.numpy as jnp
import numpy as np
from jax import lax

SURF_ORDER = 6
NCOEF = 456
RANK = 64
LEVELS = 2
P_CAP = 128
NDIR = 316
SIDE = 4
LEAF_DEV = 64
BOX_DEV = 73
NROOT = 32
LEAVES = 16384
POINT_SLOT_TOTAL = 2097152
N_MORTON = 256


def set_ends(values, stream_key, low, largest):
    shape = values.shape
    index_at = [jax.random.randint(jax.random.fold_in(stream_key, axis), (), 0, shape[axis]) for axis in range(len(shape))]
    values = values.at[tuple(index_at)].set(low)
    longest = shape.index(max(shape))
    index_at[longest] = (index_at[longest] + 1) % shape[longest]
    return values.at[tuple(index_at)].set(largest)


def level_of(rng, dims, cuts, least, high):
    gain, own = 1.0, jax.random.fold_in(rng, 6)
    for dim, parts in cuts:
        draws = jnp.exp(jax.random.uniform(jax.random.fold_in(own, dim), (parts,), jnp.float32, least / len(cuts), high / len(cuts)))
        gain = gain * jnp.repeat(draws, dims[dim] // parts).reshape([-1 if axis == dim else 1 for axis in range(len(dims))])
    return gain


def bell_draw(own_key, shape, deviation, reach, split=(), held_as=jnp.bfloat16):
    drawn = jax.random.normal(own_key, shape, jnp.float32) * deviation
    if len(split) > 0:
        drawn = level_of(own_key, shape, split, -0.22, 0.18) * drawn
    return jnp.clip(drawn, min=-reach, max=reach).astype(held_as)


def setup_inputs(seed: int = 0) -> dict:
    key_list = jax.random.split(jax.random.key(seed), 9)
    offsets = jnp.clip(jax.random.uniform(key_list[0], (3, POINT_SLOT_TOTAL), jnp.float32, -0.5, 0.5) * level_of(key_list[0], (3, POINT_SLOT_TOTAL), ((1, 256),), -0.4, 0.0), -0.5, 0.5)
    forces = bell_draw(key_list[1], (3, POINT_SLOT_TOTAL), 1.0, 6.0, ((1, 256),), jnp.float32)
    counts = set_ends(jax.random.randint(key_list[2], (LEAVES,), 1, P_CAP + 1), jax.random.fold_in(key_list[2], 1), 1, P_CAP).astype(jnp.int32)
    uc2ue = bell_draw(key_list[3], (NCOEF, NCOEF), NCOEF ** -0.5, 0.25, (), jnp.float32)
    m2m_ops = bell_draw(key_list[4], (8, NCOEF, NCOEF), (8 * NCOEF) ** -0.5, 0.09375, (), jnp.float32)
    compress = bell_draw(key_list[5], (NCOEF, RANK), NCOEF ** -0.5, 0.25, (), jnp.float32)
    m2l_ops = bell_draw(key_list[6], (NDIR, RANK, RANK), (189 * RANK) ** -0.5, 0.0546875)
    root_ops = bell_draw(key_list[7], (2 * NROOT - 1, RANK, RANK), (RANK * (N_MORTON // 8)) ** -0.5, 0.125)
    return dict(offsets=offsets, forces=forces, counts=counts, uc2ue=uc2ue, m2m_ops=m2m_ops, compress=compress, m2l_ops=m2l_ops, root_ops=root_ops)


precise = lax.Precision.HIGHEST
check_radius = 1.475

def surface_points():
    tick_values = np.linspace(-1.0, 1.0, SURF_ORDER)
    chosen = []
    for along_x in range(SURF_ORDER):
        for along_y in range(SURF_ORDER):
            for along_z in range(SURF_ORDER):
                if min(along_x, along_y, along_z) == 0 or max(along_x, along_y, along_z) == SURF_ORDER - 1:
                    chosen.append((tick_values[along_x], tick_values[along_y], tick_values[along_z]))
    return check_radius * np.array(chosen).T

def direction_lookup():
    direction_list = []
    for step_x in range(-3, 4):
        for step_y in range(-3, 4):
            for step_z in range(-3, 4):
                if max(abs(step_x), abs(step_y), abs(step_z)) >= 2:
                    direction_list.append((step_x, step_y, step_z))
    lookup = {}
    for position, entry in enumerate(direction_list):
        lookup[entry] = position
    index_table = np.full((216, 8), len(direction_list), dtype=np.int32)
    for along_x in range(6):
        for along_y in range(6):
            for along_z in range(6):
                for oddness_along_x in range(2):
                    for parity_y in range(2):
                        for oddness_along_z in range(2):
                            entry = (along_x - 2 - oddness_along_x, along_y - 2 - parity_y, along_z - 2 - oddness_along_z)
                            if entry in lookup:
                                index_table[(along_x * 6 + along_y) * 6 + along_z, (oddness_along_x * 2 + parity_y) * 2 + oddness_along_z] = lookup[entry]
    return index_table

def leaf_potentials(offsets, forces, counts):
    slot_ids = lax.broadcasted_iota(jnp.int32, (counts.shape[0], P_CAP), 1)
    live_mask = (slot_ids < counts[:, None]).astype(jnp.float32)
    masked = forces * live_mask[None]
    targets = jnp.asarray(surface_points(), dtype=jnp.float32)
    separation = targets[:, None, None, :] - offsets[..., None]
    inverse = lax.rsqrt(lax.optimization_barrier(jnp.sum(separation * separation, axis=0)))
    projected_values = lax.optimization_barrier(jnp.sum(separation * masked[..., None], axis=0))
    velocity = masked[..., None] * inverse[None] + separation * (projected_values * inverse * inverse * inverse)[None]
    total_sum = lax.optimization_barrier(jnp.sum(velocity, axis=2))
    return jnp.transpose(total_sum, (1, 0, 2)).reshape(counts.shape[0], NCOEF)

def merge_children(density, m2m_ops):
    half_side = density.shape[0] // 2
    children = density.reshape(half_side, 2, half_side, 2, half_side, 2, NCOEF)
    octants = m2m_ops.reshape(2, 2, 2, NCOEF, NCOEF)
    return jnp.einsum('apbqcrx,pqrxy->abcy', children, octants, precision=precise)

def upward_tree(offsets, forces, counts, uc2ue, m2m_ops):
    check = leaf_potentials(offsets.reshape(3, LEAF_DEV, P_CAP), forces.reshape(3, LEAF_DEV, P_CAP), counts)
    density = jnp.dot(check, uc2ue, precision=precise, preferred_element_type=jnp.float32)
    density = density.reshape(SIDE, SIDE, SIDE, NCOEF)
    levels = [density]
    for level_id in range(LEVELS):
        density = merge_children(density, m2m_ops)
        levels.insert(0, density)
    return levels

def shrink(density, compress):
    return jnp.dot(density, compress, precision=precise, preferred_element_type=jnp.float32).astype(jnp.bfloat16)

def interaction_matrix(m2l_ops):
    padded_ops = jnp.concatenate([m2l_ops, jnp.zeros((1, RANK, RANK), m2l_ops.dtype)], axis=0)
    picked = padded_ops[jnp.asarray(direction_lookup())]
    return jnp.transpose(picked, (0, 2, 1, 3)).reshape(216 * RANK, 8 * RANK)

def neighbourhood(window):
    gathered = window
    for axis_number in range(3):
        count_here = (gathered.shape[axis_number] - 4) // 2
        pieces = [lax.slice_in_dim(gathered, start_offset, start_offset + 2 * count_here - 1, 2, axis_number) for start_offset in range(6)]
        gathered = jnp.stack(pieces, axis=-2)
    parents = gathered.shape[0] * gathered.shape[1] * gathered.shape[2]
    return gathered.reshape(parents, 216 * RANK)

def spread_children(products, parent_shape):
    arranged = products.reshape(parent_shape[0], parent_shape[1], parent_shape[2], 2, 2, 2, RANK)
    arranged = jnp.transpose(arranged, (0, 3, 1, 4, 2, 5, 6))
    return arranged.reshape(2 * parent_shape[0], 2 * parent_shape[1], 2 * parent_shape[2], RANK)

def to_grid(stacked, side_boxes):
    columns_x = N_MORTON // 4
    arranged = stacked.reshape(columns_x, 2, 2, side_boxes, side_boxes, side_boxes, RANK)
    arranged = jnp.transpose(arranged, (0, 3, 1, 4, 2, 5, 6))
    return arranged.reshape(columns_x * side_boxes, 2 * side_boxes, 2 * side_boxes, RANK)

def from_grid(grid_values, side_boxes):
    columns_x = N_MORTON // 4
    arranged = grid_values.reshape(columns_x, side_boxes, 2, side_boxes, 2, side_boxes, RANK)
    arranged = jnp.transpose(arranged, (0, 2, 4, 1, 3, 5, 6))
    return arranged.reshape(N_MORTON, side_boxes * side_boxes * side_boxes, RANK)

def level_locals(multipole_grid, weights):
    cross_side = multipole_grid.shape[1]
    padded = jnp.pad(multipole_grid, ((2, 2), (2, 2), (2, 2), (0, 0))).astype(jnp.float32)

    def one_root(root_id):
        window = lax.dynamic_slice_in_dim(padded, root_id * cross_side, cross_side + 4, 0)
        products = jnp.dot(neighbourhood(window), weights, precision=precise)
        half_side = cross_side // 2
        return spread_children(products, (half_side, half_side, half_side))
    blocks = lax.map(one_root, jnp.arange(NROOT, dtype=jnp.int32))
    return blocks.reshape(NROOT * cross_side, cross_side, cross_side, RANK)

def root_locals(root_multipoles, root_ops):
    blank = jnp.zeros((NROOT, RANK), jnp.float32)
    padded = jnp.concatenate([blank, root_multipoles.astype(jnp.float32), blank], axis=0)

    def accumulate(step_index, running):
        distance = (step_index - (NROOT - 1)).astype(jnp.int32)
        source = lax.dynamic_slice_in_dim(padded, (NROOT + distance).astype(jnp.int32), NROOT, 0)
        weight = jnp.where(jnp.abs(distance) >= 2, 1.0, 0.0).astype(jnp.float32)
        root_matrix = root_ops[step_index].astype(jnp.float32)
        return running + weight * jnp.dot(source, root_matrix, precision=precise)
    return lax.fori_loop(0, 2 * NROOT - 1, accumulate, jnp.zeros((NROOT, RANK), jnp.float32))

def reference(offsets, forces, counts, uc2ue, m2m_ops, compress, m2l_ops, root_ops):
    split_offsets = jnp.transpose(offsets.reshape(3, N_MORTON, LEAF_DEV * P_CAP), (1, 0, 2))
    split_forces = jnp.transpose(forces.reshape(3, N_MORTON, LEAF_DEV * P_CAP), (1, 0, 2))
    split_counts = counts.reshape(N_MORTON, LEAF_DEV)

    def device_pass(inputs):
        levels = upward_tree(inputs[0], inputs[1], inputs[2], uc2ue, m2m_ops)
        multipoles = tuple((shrink(level_values, compress) for level_values in levels))
        return (multipoles, levels[0].reshape(NCOEF))
    multipoles, device_density = lax.map(device_pass, (split_offsets, split_forces, split_counts))
    weights = interaction_matrix(m2l_ops).astype(jnp.float32)
    level_count = []
    for level_id in range(LEVELS + 1):
        side_boxes = 2 ** level_id
        grid_values = level_locals(to_grid(multipoles[level_id], side_boxes), weights)
        level_count.append(from_grid(grid_values, side_boxes))
    local_boxes = jnp.concatenate(level_count, axis=1).reshape(N_MORTON * BOX_DEV, RANK)
    octants = m2m_ops.reshape(2, 2, 2, NCOEF, NCOEF)
    root_density = jnp.einsum('rpqsx,pqsxy->ry', device_density.reshape(NROOT, 2, 2, 2, NCOEF), octants, precision=precise)
    local_roots = root_locals(shrink(root_density, compress), root_ops)
    return (local_boxes, local_roots)
```

```python
import functools

import jax
import jax.numpy as jnp
import ml_dtypes
import numpy as np
from jax import lax
from jax.experimental import pallas as pl
from jax.experimental.pallas import tpu as pltpu
from jax.sharding import PartitionSpec as P

SURF_ORDER = 6
NQ = 152
NCOEF = 456
RANK = 64
P_CAP = 128
LEAF_DEV = 64
BOX_DEV = 73
NROOT = 32
AXIS = "morton"
CHECK_RADIUS = 1.475
LEAF_UNROLL = 4

F32 = jnp.float32
BF16 = jnp.bfloat16


def surface_points():
    ticks = np.linspace(-1.0, 1.0, SURF_ORDER)
    last = SURF_ORDER - 1
    chosen = []
    for i in range(SURF_ORDER):
        for j in range(SURF_ORDER):
            for k in range(SURF_ORDER):
                if min(i, j, k) == 0 or max(i, j, k) == last:
                    chosen.append((ticks[i], ticks[j], ticks[k]))
    return CHECK_RADIUS * np.array(chosen).T


def direction_index():
    found = {}
    for u in range(-3, 4):
        for v in range(-3, 4):
            for w in range(-3, 4):
                if max(abs(u), abs(v), abs(w)) >= 2:
                    found[(u, v, w)] = len(found)
    return found


DIRS = direction_index()


def leaf_order():
    table = np.zeros((64, 64), np.float32)
    for leaf in range(64):
        x, y, z = leaf // 16, leaf // 4 % 4, leaf % 4
        octant = (x % 2) * 4 + (y % 2) * 2 + z % 2
        parent = (x // 2) * 4 + (y // 2) * 2 + z // 2
        table[leaf, octant * 8 + parent] = 1.0
    return table.astype(ml_dtypes.bfloat16)


def reachable(shift, target):
    return not (shift == -3 and target % 2 == 0) and not (shift == 3 and target % 2 == 1)


def cross_section_picks():
    table = np.zeros((4, 49 * 32, 128), np.float32)
    for place in range(4):
        y_bit, z_bit = place // 2, place % 2
        for pair in range(49):
            v, w = pair // 7 - 3, pair % 7 - 3
            for side, first, copies in ((4, 0, 1), (2, 16, 2)):
                for y in range(side):
                    for z in range(side):
                        if not (reachable(v, y) and reachable(w, z)):
                            continue
                        gy, gz = side * y_bit + y + v, side * z_bit + z + w
                        if not (0 <= gy < 2 * side and 0 <= gz < 2 * side):
                            continue
                        owner = (gy // side) * 2 + gz // side
                        source = (owner ^ place) * 32 + first + (gy % side) * side + gz % side
                        for copy in range(copies):
                            table[place, pair * 32 + first + 4 * copy + y * side + z, source] = 1.0
    return table.astype(ml_dtypes.bfloat16)


def device_level_table():
    rows = np.zeros((8, 24), np.int32)
    for place in range(8):
        parity, y_bit, z_bit = place // 4, place // 2 % 2, place % 2
        columns = (-2, 2, 3) if parity == 0 else (-2, -1, 3)
        for n, column in enumerate(columns):
            for other in range(4):
                entry = (column - parity, other // 2 - y_bit, other % 2 - z_bit)
                rows[place, n * 4 + other] = DIRS[entry]
            rows[place, 12 + n] = column
    return rows


def split(x):
    high = x.astype(BF16).astype(F32)
    return high, x - high


def stacked(x):
    high, low = split(x)
    return jnp.concatenate([high, low], axis=0).astype(BF16)


def dot(a, b):
    return jnp.dot(a, b, preferred_element_type=F32)


def product(x, w_high, w_low):
    rows = x.shape[0]
    both = stacked(x)
    top = dot(both, w_high)
    rest = dot(both, w_low)
    return top[:rows] + (top[rows:] + rest[:rows])


def upward_kernel(
    offsets, forces, counts, surface, order, uc2ue, m2m_hbm, compress, shared, block,
    m2m, m2m_high, m2m_low, check, sem,
):
    fetch = pltpu.make_async_copy(m2m_hbm, m2m, sem)
    fetch.start()
    slots = lax.broadcasted_iota(jnp.int32, (1, P_CAP), 1)
    zero = jnp.zeros((1, P_CAP), F32)
    one = jnp.ones((1, P_CAP), F32)

    def leaf(l, carry):
        columns = pl.ds(pl.multiple_of(l * P_CAP, P_CAP), P_CAP)
        u = offsets[:, columns]
        live = (slots < counts[l]).astype(F32)
        f = forces[:, columns] * live
        r = [surface[s] - u[s : s + 1] for s in range(3)]
        inverse = lax.rsqrt(r[0] * r[0] + r[1] * r[1] + r[2] * r[2])
        along = r[0] * f[0:1] + r[1] * f[1:2] + r[2] * f[2:3]
        pulled = along * (inverse * inverse * inverse)
        both = jnp.concatenate([inverse, pulled], axis=1)
        high, low = split(both)
        left = jnp.concatenate(
            [jnp.concatenate([f, zero], axis=0), jnp.concatenate([-u, one], axis=0)], axis=1
        )
        left = stacked(left)
        nt = (((1,), (1,)), ((), ()))
        top = lax.dot_general(left, high.astype(BF16), nt, preferred_element_type=F32)
        rest = lax.dot_general(left, low.astype(BF16), nt, preferred_element_type=F32)
        sums = top[0:4] + (top[4:8] + rest[0:4])
        octant = (l >> 4 & 1) * 4 + (l >> 2 & 1) * 2 + (l & 1)
        parent = (l >> 5 & 1) * 4 + (l >> 3 & 1) * 2 + (l >> 1 & 1)
        check[pl.ds(octant * 8 + parent, 1)] = sums[None]
        return carry

    lax.fori_loop(0, LEAF_DEV, leaf, 0, unroll=LEAF_UNROLL)

    points = surface[3][:, :]
    density = jnp.zeros((LEAF_DEV, NCOEF), F32)
    for s in range(3):
        rows = check[:, s, :] + check[:, 3, :] * points[s : s + 1, :]
        w_high, w_low = split(uc2ue[s * NQ : (s + 1) * NQ, :])
        density = density + product(rows, w_high.astype(BF16), w_low.astype(BF16))
    shrink = compress[...]
    shrink = jnp.concatenate([shrink, shrink], axis=1)
    s_high, s_low = split(shrink)
    s_high, s_low = s_high.astype(BF16), s_low.astype(BF16)
    lower = lax.broadcasted_iota(jnp.int32, (1, 128), 1) < RANK
    leaves = product(density, s_high, s_low).astype(BF16)
    leaves = dot(order[...], leaves)
    block[0:16, 0:128] = jnp.where(lower, leaves[0:16], leaves[16:32]).astype(BF16)
    block[0:16, 128:256] = jnp.where(lower, leaves[32:48], leaves[48:64]).astype(BF16)

    fetch.wait()
    parents = jnp.zeros((8, NCOEF), F32)
    for o in range(8):
        w_high, w_low = split(m2m[o])
        w_high, w_low = w_high.astype(BF16), w_low.astype(BF16)
        m2m_high[o] = w_high
        m2m_low[o] = w_low
        parents = parents + product(density[o * 8 : o * 8 + 8], w_high, w_low)
    middle = product(parents, s_high, s_low).astype(BF16).astype(F32)
    middle = jnp.where(lower, middle[0:4], middle[4:8])

    def one_row(x, w_high, w_low):
        high, low = split(x)
        row = lax.broadcasted_iota(jnp.int32, (8, 1), 0)
        both = jnp.where(row == 0, high, jnp.where(row == 1, low, 0.0)).astype(BF16)
        top = dot(both, w_high)
        rest = dot(both, w_low)
        return top[0:1] + (top[1:2] + rest[0:1])

    device = jnp.zeros((1, NCOEF), F32)
    for o in range(8):
        device = device + one_row(parents[o : o + 1], m2m_high[o], m2m_low[o])
    own = one_row(device, s_high, s_low).astype(BF16).astype(F32)
    octant = lax.axis_index(AXIS) % 8
    above = one_row(device, m2m_high[octant], m2m_low[octant])
    above = one_row(above, s_high, s_low)
    shared[...] = jnp.broadcast_to(jnp.where(lower, own, above), shared.shape)
    middle = jnp.concatenate([middle, jnp.zeros((12, 128), F32)], axis=0).astype(BF16)
    block[16:32, 0:128] = middle
    block[16:32, 128:256] = middle


def far_kernel(
    table, own, below, above, shared, picks_hbm, m2l, root_ops, boxes, roots,
    picks, near, base, shifted, sem,
):
    me = lax.axis_index(AXIS)
    place = me % 4
    fetch = pltpu.make_async_copy(picks_hbm.at[place], picks, sem)
    fetch.start()

    lanes = lax.broadcasted_iota(jnp.int32, (1, 128), 1)
    lower = lanes < RANK
    gathered = shared[...]
    high_half = jnp.sum(gathered.reshape(NROOT, 8, 128), axis=1).astype(BF16).astype(F32)
    low_half = pltpu.roll(high_half, RANK, 1)
    base[...] = jnp.zeros(base.shape, F32)
    shifted[...] = jnp.zeros(shifted.shape, F32)
    base[32:64, :] = jnp.where(lower, low_half, 0.0)
    shifted[31:63, :] = jnp.where(lower, 0.0, high_half)
    base[...] = base[...] + shifted[...]
    total = jnp.zeros((NROOT, RANK), F32)
    for distance in range(-31, 32, 2):
        if distance == -1:
            continue
        source = base[32 + distance : 64 + distance, :]
        first = distance + NROOT - 1
        if distance == 1:
            source = jnp.where(lower, 0.0, source)
        if distance == 31:
            total = total + dot(source[:, :RANK].astype(BF16), root_ops[first])
            continue
        operator = jnp.concatenate([root_ops[first], root_ops[first + 1]], axis=0)
        total = total + dot(source.astype(BF16), operator)
    roots[...] = total

    row_of = me % 8
    first_column = me // 8 * 2
    columns_total = lax.axis_size(AXIS) // 4
    far = jnp.zeros((8, RANK), F32)
    for n in range(3):
        column = first_column + table[row_of, 12 + n]
        inside = jnp.logical_and(column >= 0, column < columns_total)
        kept = jnp.where(inside, 1.0, 0.0).astype(F32)
        start = jnp.clip(column, 0, columns_total - 1) * 4
        for other in range(4):
            source = shared[pl.ds(start + other, 1), :][:, :RANK] * kept
            source = jnp.broadcast_to(source, (8, RANK)).astype(BF16)
            far = far + dot(source, m2l[table[row_of, n * 4 + other]])
    boxes[0:1, :] = far[0:1]

    x01, x23, x45, x67 = below[...], own[:, 0:128], own[:, 128:256], above[...]

    def crossed(a, b):
        return jnp.where(lower, pltpu.roll(a, RANK, 1), pltpu.roll(b, RANK, 1))

    x01, x23, x45, x67 = (x.astype(F32) for x in (x01, x23, x45, x67))
    none = jnp.zeros_like(x01)
    blocks = [
        x01, x23, x45, x67,
        crossed(x01, x23), crossed(x23, x45), crossed(x45, x67),
        crossed(none, x01), crossed(none, x23), crossed(x45, none), crossed(x67, none),
    ]
    wide = jnp.concatenate(blocks, axis=1).astype(BF16)
    fetch.wait()
    near[...] = dot(picks[...], wide).astype(BF16)

    def part(pair, rows, which):
        if which is None:
            return jnp.zeros((16, 128), BF16)
        first = pair * 32 + rows
        return near[first : first + 16, which * 128 : which * 128 + 128]

    even = {0: (7, 4, 5, 9), 1: (8, 5, 6, 10)}
    odd = {0: (0, 1, 2, None), 1: (1, 2, 3, None)}
    even_far = {0: (7, 2), 1: (8, 3)}
    odd_far = {0: (0, 9), 1: (1, 10)}
    level1 = ((7, 4, 6, 10), (0, 1, 3, None))
    level1_far = ((7, 3), (0, 10))
    first_rows = lax.broadcasted_iota(jnp.int32, (16, 128), 0) < 4
    total = jnp.zeros((80, RANK), F32)
    for pair in range(49):
        v, w = pair // 7 - 3, pair % 7 - 3
        close = max(abs(v), abs(w)) < 2
        shifts = (-3, -2, 2, 3) if close else range(-3, 4)
        e, o, l1 = (even_far, odd_far, level1_far) if close else (even, odd, level1)
        rows = []
        for halves in (e, o):
            for a in range(2):
                rows.append(jnp.concatenate([part(pair, 0, k) for k in halves[a]], axis=1))
        both = [
            jnp.where(first_rows, part(pair, 16, a).astype(F32), part(pair, 16, b).astype(F32)).astype(BF16)
            for a, b in zip(*l1)
        ]
        rows.append(jnp.concatenate(both, axis=1))
        left = jnp.concatenate(rows, axis=0)
        operator = [m2l[DIRS[(u, v, w)]] for u in shifts]
        if not close:
            left = left[:, : 7 * RANK]
        total = total + dot(left, jnp.concatenate(operator, axis=0))
    boxes[1:9, :] = total[64:72]
    for p in range(2):
        for a in range(2):
            x = 2 * a + p
            first = (p * 2 + a) * 16
            boxes[9 + 16 * x : 25 + 16 * x, :] = total[first : first + 16]


def whole(space=pltpu.VMEM):
    return pl.BlockSpec(memory_space=space)


def upward(offsets, forces, counts, uc2ue, m2m_ops, compress):
    devices = lax.axis_size(AXIS)
    points = surface_points().astype(np.float32)
    spread = np.zeros((4, NQ, P_CAP), np.float32)
    spread[:3] = points[:, :, None]
    rows = np.zeros((8, NQ), np.float32)
    rows[:3] = points

    def kernel(off, frc, cnt, surf, pts, order, uc, m2m_hbm, comp, shared, block, *scratch):
        surface = [surf.at[0], surf.at[1], surf.at[2], pts]
        wrapped = Surface(surface)
        upward_kernel(off, frc, cnt, wrapped, order, uc, m2m_hbm, comp, shared, block, *scratch)

    return pl.pallas_call(
        kernel,
        out_shape=(
            jax.ShapeDtypeStruct((devices, 128), F32),
            jax.ShapeDtypeStruct((32, 256), BF16),
        ),
        in_specs=[
            whole(), whole(), whole(pltpu.SMEM), whole(), whole(), whole(), whole(),
            whole(pl.ANY), whole(),
        ],
        out_specs=(whole(), whole()),
        scratch_shapes=[
            pltpu.VMEM((8, NCOEF, NCOEF), F32),
            pltpu.VMEM((8, NCOEF, NCOEF), BF16),
            pltpu.VMEM((8, NCOEF, NCOEF), BF16),
            pltpu.VMEM((LEAF_DEV, 4, NQ), F32),
            pltpu.SemaphoreType.DMA,
        ],
        compiler_params=pltpu.CompilerParams(vmem_limit_bytes=40 * 2**20),
        name="upward",
    )(
        offsets, forces, counts, jnp.asarray(spread[:3]), jnp.asarray(rows),
        jnp.asarray(leaf_order()), uc2ue, m2m_ops, compress,
    )


class Surface:
    def __init__(self, refs):
        self.refs = refs

    def __getitem__(self, s):
        return self.refs[s][...] if s < 3 else self.refs[3]


def far_field(own, below, above, shared, m2l_ops, root_ops):
    return pl.pallas_call(
        far_kernel,
        out_shape=(
            jax.ShapeDtypeStruct((BOX_DEV, RANK), F32),
            jax.ShapeDtypeStruct((NROOT, RANK), F32),
        ),
        in_specs=[
            whole(pltpu.SMEM), whole(), whole(), whole(), whole(), whole(pl.ANY), whole(), whole(),
        ],
        out_specs=(whole(), whole()),
        scratch_shapes=[
            pltpu.VMEM((49 * 32, 128), BF16),
            pltpu.VMEM((49 * 32, 11 * 128), BF16),
            pltpu.VMEM((96, 128), F32),
            pltpu.VMEM((96, 128), F32),
            pltpu.SemaphoreType.DMA,
        ],
        compiler_params=pltpu.CompilerParams(vmem_limit_bytes=40 * 2**20),
        name="far_field",
    )(
        jnp.asarray(device_level_table()), own, below, above, shared,
        jnp.asarray(cross_section_picks()), m2l_ops, root_ops,
    )


def swapped(value, mask):
    devices = lax.axis_size(AXIS)
    return lax.ppermute(value, AXIS, [(s, s ^ mask) for s in range(devices)])


def swapped_between(value, unit):
    devices = lax.axis_size(AXIS)
    pairs = []
    for s in range(devices):
        b, r = divmod(s, unit)
        t = b + 1 if b % 2 == 1 else b - 1
        if 0 <= t < devices // unit:
            pairs.append((s, t * unit + r))
    return lax.ppermute(value, AXIS, pairs)


def body(offsets, forces, counts, uc2ue, m2m_ops, compress, m2l_ops, root_ops):
    me = lax.axis_index(AXIS)
    shared, block = upward(offsets, forces, counts, uc2ue, m2m_ops, compress)
    shared = lax.all_to_all(shared, AXIS, 0, 0, tiled=True)
    two = jnp.concatenate([block, swapped(block, 1)], axis=0)
    own = jnp.concatenate([two, swapped(two, 2)], axis=0)
    pair = swapped(own, 6)
    pair = jnp.concatenate([pair[64:], pair[:64]], axis=0)
    is_upper = me // 4 % 2 == 1
    root_even = me // 8 % 2 == 0
    upper_rim = jnp.where(is_upper, own[:, 128:], pair[:, 128:])
    lower_rim = jnp.where(is_upper, pair[:, :128], own[:, :128])
    inner = swapped(jnp.where(root_even, upper_rim, lower_rim), 8)
    outer = swapped_between(jnp.where(root_even, lower_rim, upper_rim), 8)
    from_below = jnp.where(root_even, outer, inner)
    from_above = jnp.where(root_even, inner, outer)
    below = jnp.where(is_upper, pair[:, 128:], from_below)
    above = jnp.where(is_upper, from_above, pair[:, :128])
    return far_field(own, below, above, shared, m2l_ops, root_ops)


def solution(mesh):
    placed = (P(None, AXIS), P(None, AXIS), P(AXIS), P(), P(), P(), P(), P())
    return jax.shard_map(
        body, mesh=mesh, in_specs=placed, out_specs=(P(AXIS, None), P()), check_vma=False
    )
```

```python
import functools

import jax
import jax.numpy as jnp
import ml_dtypes
import numpy as np
from jax import lax
from jax.experimental import pallas as pl
from jax.experimental.pallas import tpu as pltpu
from jax.sharding import PartitionSpec as P

SURF_ORDER = 6
NQ = 152
NCOEF = 456
RANK = 64
P_CAP = 128
LEAF_DEV = 64
BOX_DEV = 73
NROOT = 32
AXIS = "morton"
CHECK_RADIUS = 1.475
LEAF_UNROLL = 4

F32 = jnp.float32
BF16 = jnp.bfloat16


def surface_points():
    ticks = np.linspace(-1.0, 1.0, SURF_ORDER)
    last = SURF_ORDER - 1
    chosen = []
    for i in range(SURF_ORDER):
        for j in range(SURF_ORDER):
            for k in range(SURF_ORDER):
                if min(i, j, k) == 0 or max(i, j, k) == last:
                    chosen.append((ticks[i], ticks[j], ticks[k]))
    return CHECK_RADIUS * np.array(chosen).T


def direction_index():
    found = {}
    for u in range(-3, 4):
        for v in range(-3, 4):
            for w in range(-3, 4):
                if max(abs(u), abs(v), abs(w)) >= 2:
                    found[(u, v, w)] = len(found)
    return found


DIRS = direction_index()


def leaf_order():
    table = np.zeros((64, 64), np.float32)
    for leaf in range(64):
        x, y, z = leaf // 16, leaf // 4 % 4, leaf % 4
        octant = (x % 2) * 4 + (y % 2) * 2 + z % 2
        parent = (x // 2) * 4 + (y // 2) * 2 + z // 2
        table[leaf, octant * 8 + parent] = 1.0
    return table.astype(ml_dtypes.bfloat16)


def reachable(shift, target):
    return not (shift == -3 and target % 2 == 0) and not (shift == 3 and target % 2 == 1)


def cross_section_picks():
    table = np.zeros((4, 49 * 32, 128), np.float32)
    for place in range(4):
        y_bit, z_bit = place // 2, place % 2
        for pair in range(49):
            v, w = pair // 7 - 3, pair % 7 - 3
            for side, first, copies in ((4, 0, 1), (2, 16, 2)):
                for y in range(side):
                    for z in range(side):
                        if not (reachable(v, y) and reachable(w, z)):
                            continue
                        gy, gz = side * y_bit + y + v, side * z_bit + z + w
                        if not (0 <= gy < 2 * side and 0 <= gz < 2 * side):
                            continue
                        owner = (gy // side) * 2 + gz // side
                        source = (owner ^ place) * 32 + first + (gy % side) * side + gz % side
                        for copy in range(copies):
                            table[place, pair * 32 + first + 4 * copy + y * side + z, source] = 1.0
    return table.astype(ml_dtypes.bfloat16)


def device_level_table():
    rows = np.zeros((8, 24), np.int32)
    for place in range(8):
        parity, y_bit, z_bit = place // 4, place // 2 % 2, place % 2
        columns = (-2, 2, 3) if parity == 0 else (-2, -1, 3)
        for n, column in enumerate(columns):
            for other in range(4):
                entry = (column - parity, other // 2 - y_bit, other % 2 - z_bit)
                rows[place, n * 4 + other] = DIRS[entry]
            rows[place, 12 + n] = column
    return rows


def split(x):
    high = x.astype(BF16).astype(F32)
    return high, x - high


def stacked(x):
    high, low = split(x)
    return jnp.concatenate([high, low], axis=0).astype(BF16)


def dot(a, b):
    return jnp.dot(a, b, preferred_element_type=F32)


def dot_nt(a, b):
    return lax.dot_general(a, b, (((1,), (1,)), ((), ())), preferred_element_type=F32)


def product(x, w_high, w_low, dot=dot):
    rows = x.shape[0]
    both = stacked(x)
    top = dot(both, w_high)
    rest = dot(both, w_low)
    return top[:rows] + (top[rows:] + rest[:rows])


def upward_kernel(
    offsets_hbm, forces_hbm, counts_hbm, surface_hbm, points_hbm, order_hbm, uc2ue_hbm, m2m_hbm,
    compress_hbm, shared, block,
    offsets, forces, counts, surface, points, order, uc2ue, m2m, compress,
    m2m_high, m2m_low, check, sems,
):
    pairs = (
        (offsets_hbm, offsets), (forces_hbm, forces), (counts_hbm, counts), (surface_hbm, surface),
        (points_hbm, points), (order_hbm, order), (uc2ue_hbm, uc2ue), (compress_hbm, compress),
        (m2m_hbm, m2m),
    )
    fetches = [pltpu.make_async_copy(a, b, sems.at[n]) for n, (a, b) in enumerate(pairs)]
    for fetch in fetches:
        fetch.start()
    for fetch in fetches[:4]:
        fetch.wait()
    slots = lax.broadcasted_iota(jnp.int32, (1, P_CAP), 1)
    zero = jnp.zeros((1, P_CAP), F32)
    one = jnp.ones((1, P_CAP), F32)

    def leaf(l, carry):
        columns = pl.ds(pl.multiple_of(l * P_CAP, P_CAP), P_CAP)
        u = offsets[:, columns]
        live = (slots < counts[l]).astype(F32)
        f = forces[:, columns] * live
        r = [surface[s] - u[s : s + 1] for s in range(3)]
        inverse = lax.rsqrt(r[0] * r[0] + r[1] * r[1] + r[2] * r[2])
        along = r[0] * f[0:1] + r[1] * f[1:2] + r[2] * f[2:3]
        pulled = along * (inverse * inverse * inverse)
        both = jnp.concatenate([inverse, pulled], axis=1)
        high, low = split(both)
        left = jnp.concatenate(
            [jnp.concatenate([f, zero], axis=0), jnp.concatenate([-u, one], axis=0)], axis=1
        )
        left = stacked(left)
        top = dot_nt(left, high.astype(BF16))
        rest = dot_nt(left, low.astype(BF16))
        sums = top[0:4] + (top[4:8] + rest[0:4])
        octant = (l >> 4 & 1) * 4 + (l >> 2 & 1) * 2 + (l & 1)
        parent = (l >> 5 & 1) * 4 + (l >> 3 & 1) * 2 + (l >> 1 & 1)
        check[pl.ds(octant * 8 + parent, 1)] = sums[None]
        return carry

    lax.fori_loop(0, LEAF_DEV, leaf, 0, unroll=LEAF_UNROLL)

    for fetch in fetches[4:8]:
        fetch.wait()
    density = jnp.zeros((LEAF_DEV, NCOEF), F32)
    for s in range(3):
        rows = check[:, s, :] + check[:, 3, :] * points[s : s + 1, :]
        w_high, w_low = split(uc2ue[s * NQ : (s + 1) * NQ, :])
        density = density + product(rows, w_high.astype(BF16), w_low.astype(BF16))
    shrink = compress[...]
    shrink = jnp.concatenate([shrink, shrink], axis=0)
    s_high, s_low = split(shrink)
    s_high, s_low = s_high.astype(BF16), s_low.astype(BF16)
    lower = lax.broadcasted_iota(jnp.int32, (1, 128), 1) < RANK
    leaves = product(density, s_high, s_low, dot_nt).astype(BF16)
    leaves = dot(order[...], leaves)
    block[0:16, 0:128] = jnp.where(lower, leaves[0:16], leaves[16:32]).astype(BF16)
    block[0:16, 128:256] = jnp.where(lower, leaves[32:48], leaves[48:64]).astype(BF16)

    fetches[8].wait()
    parents = jnp.zeros((8, NCOEF), F32)
    for o in range(8):
        w_high, w_low = split(m2m[o])
        w_high, w_low = w_high.astype(BF16), w_low.astype(BF16)
        m2m_high[o] = w_high
        m2m_low[o] = w_low
        parents = parents + product(density[o * 8 : o * 8 + 8], w_high, w_low)
    middle = product(parents, s_high, s_low, dot_nt).astype(BF16).astype(F32)
    middle = jnp.where(lower, middle[0:4], middle[4:8])

    def one_row(x, w_high, w_low, dot=dot):
        high, low = split(x)
        row = lax.broadcasted_iota(jnp.int32, (8, 1), 0)
        both = jnp.where(row == 0, high, jnp.where(row == 1, low, 0.0)).astype(BF16)
        top = dot(both, w_high)
        rest = dot(both, w_low)
        return top[0:1] + (top[1:2] + rest[0:1])

    device = jnp.zeros((1, NCOEF), F32)
    for o in range(8):
        device = device + one_row(parents[o : o + 1], m2m_high[o], m2m_low[o])
    own = one_row(device, s_high, s_low, dot_nt).astype(BF16).astype(F32)
    octant = lax.axis_index(AXIS) % 8
    above = one_row(device, m2m_high[octant], m2m_low[octant])
    above = one_row(above, s_high, s_low, dot_nt)
    shared[...] = jnp.broadcast_to(jnp.where(lower, own, above), shared.shape)
    middle = jnp.concatenate([middle, jnp.zeros((12, 128), F32)], axis=0).astype(BF16)
    block[16:32, 0:128] = middle
    block[16:32, 128:256] = middle


def operators_kernel(source_hbm, out, source, turned, sem):
    fetch = pltpu.make_async_copy(source_hbm, source, sem)
    fetch.start()
    directions = source.shape[2]
    rows = (directions + 7) // 8 * 8
    pitch = turned.shape[1] // 16
    shape = (rows, directions)
    unit = lax.broadcasted_iota(jnp.int32, shape, 0) == lax.broadcasted_iota(jnp.int32, shape, 1)
    unit = unit.astype(F32).astype(BF16)
    fetch.wait()
    for g in range(16):
        four = jnp.concatenate([source[g + 16 * part] for part in range(4)], axis=0)
        moved = dot_nt(unit, four)
        for half in range(2):
            turned[half, g * pitch : g * pitch + rows, :] = moved[:, half * 128 : half * 128 + 128]
    for d in range(directions):
        parts = []
        for half in range(2):
            pair = turned[half, pl.ds(d, 16, stride=pitch), :]
            parts += [pair, pltpu.roll(pair, RANK, 1)]
        out[d] = jnp.concatenate(parts, axis=0)[:, :RANK].astype(BF16)


def far_kernel(table, own, below, above, picks_hbm, m2l, boxes, device_ops, picks, near, sem):
    me = lax.axis_index(AXIS)
    fetch = pltpu.make_async_copy(picks_hbm.at[me % 4], picks, sem)
    fetch.start()
    lower = lax.broadcasted_iota(jnp.int32, (1, 128), 1) < RANK
    for n in range(12):
        device_ops[n] = m2l[table[me % 8, n]]

    x01, x23, x45, x67 = below[...], own[:, 0:128], own[:, 128:256], above[...]

    def crossed(a, b):
        return jnp.where(lower, pltpu.roll(a, RANK, 1), pltpu.roll(b, RANK, 1))

    x01, x23, x45, x67 = (x.astype(F32) for x in (x01, x23, x45, x67))
    none = jnp.zeros_like(x01)
    blocks = [
        x01, x23, x45, x67,
        crossed(x01, x23), crossed(x23, x45), crossed(x45, x67),
        crossed(none, x01), crossed(none, x23), crossed(x45, none), crossed(x67, none),
    ]
    wide = jnp.concatenate(blocks, axis=1).astype(BF16)
    fetch.wait()
    near[...] = dot(picks[...], wide).astype(BF16)

    def part(pair, rows, which):
        if which is None:
            return jnp.zeros((16, 128), BF16)
        first = pair * 32 + rows
        return near[first : first + 16, which * 128 : which * 128 + 128]

    even = {0: (7, 4, 5, 9), 1: (8, 5, 6, 10)}
    odd = {0: (0, 1, 2, None), 1: (1, 2, 3, None)}
    even_far = {0: (7, 2), 1: (8, 3)}
    odd_far = {0: (0, 9), 1: (1, 10)}
    level1 = ((7, 4, 6, 10), (0, 1, 3, None))
    level1_far = ((7, 3), (0, 10))
    first_rows = lax.broadcasted_iota(jnp.int32, (16, 128), 0) < 4
    total = jnp.zeros((80, RANK), F32)
    for pair in range(49):
        v, w = pair // 7 - 3, pair % 7 - 3
        close = max(abs(v), abs(w)) < 2
        shifts = (-3, -2, 2, 3) if close else range(-3, 4)
        e, o, l1 = (even_far, odd_far, level1_far) if close else (even, odd, level1)
        rows = []
        for halves in (e, o):
            for a in range(2):
                rows.append(jnp.concatenate([part(pair, 0, k) for k in halves[a]], axis=1))
        both = [
            jnp.where(first_rows, part(pair, 16, a).astype(F32), part(pair, 16, b).astype(F32)).astype(BF16)
            for a, b in zip(*l1)
        ]
        rows.append(jnp.concatenate(both, axis=1))
        left = jnp.concatenate(rows, axis=0)
        operator = [m2l[DIRS[(u, v, w)]] for u in shifts]
        if not close:
            left = left[:, : 7 * RANK]
        total = total + dot(left, jnp.concatenate(operator, axis=0))
    boxes[...] = jnp.zeros(boxes.shape, F32)
    boxes[1:9, :] = total[64:72]
    for p in range(2):
        for a in range(2):
            x = 2 * a + p
            first = (p * 2 + a) * 16
            boxes[9 + 16 * x : 25 + 16 * x, :] = total[first : first + 16]


def top_kernel(table, partial, device_ops, shared, root_ops, boxes, roots, base, shifted, turned):
    me = lax.axis_index(AXIS)
    lower = lax.broadcasted_iota(jnp.int32, (1, 128), 1) < RANK
    gathered = shared[...]
    high_half = jnp.sum(gathered.reshape(NROOT, 8, 128), axis=1).astype(BF16).astype(F32)
    low_half = pltpu.roll(high_half, RANK, 1)
    base[...] = jnp.zeros(base.shape, F32)
    shifted[...] = jnp.zeros(shifted.shape, F32)
    base[32:64, :] = jnp.where(lower, low_half, 0.0)
    shifted[31:63, :] = jnp.where(lower, 0.0, high_half)
    base[...] = base[...] + shifted[...]
    total = jnp.zeros((NROOT, RANK), F32)
    for distance in range(-31, 32, 2):
        if distance == -1:
            continue
        source = base[32 + distance : 64 + distance, :]
        first = distance + NROOT - 1
        if distance == 1:
            source = jnp.where(lower, 0.0, source)
        if distance == 31:
            total = total + dot(source[:, :RANK].astype(BF16), root_ops[first])
            continue
        operator = jnp.concatenate([root_ops[first], root_ops[first + 1]], axis=0)
        total = total + dot(source.astype(BF16), operator)
    roots[...] = total

    first_column = me // 8 * 2
    columns_total = lax.axis_size(AXIS) // 4
    far = jnp.zeros((8, RANK), F32)
    for n in range(3):
        column = first_column + table[me % 8, 12 + n]
        inside = jnp.logical_and(column >= 0, column < columns_total)
        kept = jnp.where(inside, 1.0, 0.0).astype(F32)
        start = jnp.clip(column, 0, columns_total - 1) * 4
        for other in range(4):
            source = shared[pl.ds(start + other, 1), :][:, :RANK] * kept
            source = jnp.broadcast_to(source, (8, RANK)).astype(BF16)
            far = far + dot(source, device_ops[n * 4 + other])
    turned[...] = jnp.zeros(turned.shape, F32)
    turned[0:80, 0:RANK] = partial[...]
    turned[0:1, 0:RANK] = far[0:1]
    boxes[...] = turned[...].T[:RANK, :BOX_DEV]


def whole(space=pltpu.VMEM):
    return pl.BlockSpec(memory_space=space)


def upward(offsets, forces, counts, uc2ue, m2m_ops, compress):
    devices = lax.axis_size(AXIS)
    points = surface_points().astype(np.float32)
    spread = np.ascontiguousarray(np.broadcast_to(points[:, :, None], (3, NQ, P_CAP)))
    rows = np.zeros((8, NQ), np.float32)
    rows[:3] = points
    operands = (
        offsets, forces, counts, jnp.asarray(spread), jnp.asarray(rows), jnp.asarray(leaf_order()),
        uc2ue, m2m_ops, compress.T,
    )
    held = [pltpu.VMEM(x.shape, x.dtype) for x in operands]
    held[2] = pltpu.SMEM(counts.shape, counts.dtype)
    return pl.pallas_call(
        upward_kernel,
        out_shape=(
            jax.ShapeDtypeStruct((devices, 128), F32),
            jax.ShapeDtypeStruct((32, 256), BF16),
        ),
        in_specs=[whole(pltpu.HBM)] * len(operands),
        out_specs=(whole(), whole()),
        scratch_shapes=held
        + [
            pltpu.VMEM((8, NCOEF, NCOEF), BF16),
            pltpu.VMEM((8, NCOEF, NCOEF), BF16),
            pltpu.VMEM((LEAF_DEV, 4, NQ), F32),
            pltpu.SemaphoreType.DMA((len(operands),)),
        ],
        compiler_params=pltpu.CompilerParams(vmem_limit_bytes=40 * 2**20),
        name="upward",
    )(*operands)


def operators(m2l_ops):
    count = m2l_ops.shape[0]
    return pl.pallas_call(
        operators_kernel,
        out_shape=jax.ShapeDtypeStruct(m2l_ops.shape, BF16),
        in_specs=[whole(pltpu.HBM)],
        out_specs=whole(),
        scratch_shapes=[
            pltpu.VMEM((RANK, RANK, count), BF16),
            pltpu.VMEM((2, 16 * (count + 5), 128), F32),
            pltpu.SemaphoreType.DMA,
        ],
        compiler_params=pltpu.CompilerParams(vmem_limit_bytes=28 * 2**20),
        name="operators",
    )(jnp.transpose(m2l_ops, (1, 2, 0)))


def far_field(table, own, below, above, m2l):
    return pl.pallas_call(
        far_kernel,
        out_shape=(
            jax.ShapeDtypeStruct((80, RANK), F32),
            jax.ShapeDtypeStruct((12, RANK, RANK), BF16),
        ),
        in_specs=[whole(pltpu.SMEM), whole(), whole(), whole(), whole(pltpu.HBM), whole()],
        out_specs=(whole(), whole()),
        scratch_shapes=[
            pltpu.VMEM((49 * 32, 128), BF16),
            pltpu.VMEM((49 * 32, 11 * 128), BF16),
            pltpu.SemaphoreType.DMA,
        ],
        compiler_params=pltpu.CompilerParams(vmem_limit_bytes=28 * 2**20),
        name="far_field",
    )(table, own, below, above, jnp.asarray(cross_section_picks()), m2l)


def top_levels(table, partial, device_ops, shared, root_ops):
    boxes, roots = pl.pallas_call(
        top_kernel,
        out_shape=(
            jax.ShapeDtypeStruct((RANK, BOX_DEV), F32),
            jax.ShapeDtypeStruct((NROOT, RANK), F32),
        ),
        in_specs=[whole(pltpu.SMEM)] + [whole()] * 4,
        out_specs=(whole(), whole()),
        scratch_shapes=[
            pltpu.VMEM((96, 128), F32),
            pltpu.VMEM((96, 128), F32),
            pltpu.VMEM((128, 128), F32),
        ],
        compiler_params=pltpu.CompilerParams(vmem_limit_bytes=16 * 2**20),
        name="top_levels",
    )(table, partial, device_ops, shared, root_ops)
    return boxes.T, roots


def swapped(value, mask):
    devices = lax.axis_size(AXIS)
    return lax.ppermute(value, AXIS, [(s, s ^ mask) for s in range(devices)])


def swapped_between(value, unit):
    devices = lax.axis_size(AXIS)
    pairs = []
    for s in range(devices):
        b, r = divmod(s, unit)
        t = b + 1 if b % 2 == 1 else b - 1
        if 0 <= t < devices // unit:
            pairs.append((s, t * unit + r))
    return lax.ppermute(value, AXIS, pairs)


def body(offsets, forces, counts, uc2ue, m2m_ops, compress, m2l_ops, root_ops):
    me = lax.axis_index(AXIS)
    shared, block = upward(offsets, forces, counts, uc2ue, m2m_ops, compress)
    shared = lax.all_to_all(shared, AXIS, 0, 0, tiled=True)
    two = jnp.concatenate([block, swapped(block, 1)], axis=0)
    own = jnp.concatenate([two, swapped(two, 2)], axis=0)
    pair = swapped(own, 6)
    pair = jnp.concatenate([pair[64:], pair[:64]], axis=0)
    is_upper = me // 4 % 2 == 1
    root_even = me // 8 % 2 == 0
    upper_rim = jnp.where(is_upper, own[:, 128:], pair[:, 128:])
    lower_rim = jnp.where(is_upper, pair[:, :128], own[:, :128])
    inner = swapped(jnp.where(root_even, upper_rim, lower_rim), 8)
    outer = swapped_between(jnp.where(root_even, lower_rim, upper_rim), 8)
    from_below = jnp.where(root_even, outer, inner)
    from_above = jnp.where(root_even, inner, outer)
    below = jnp.where(is_upper, pair[:, 128:], from_below)
    above = jnp.where(is_upper, from_above, pair[:, :128])
    table = jnp.asarray(device_level_table())
    partial, device_ops = far_field(table, own, below, above, operators(m2l_ops))
    return top_levels(table, partial, device_ops, shared, root_ops)


def solution(mesh):
    placed = (P(None, AXIS), P(None, AXIS), P(AXIS), P(), P(), P(), P(), P())
    return jax.shard_map(
        body, mesh=mesh, in_specs=placed, out_specs=(P(AXIS, None), P()), check_vma=False
    )
```

```python
import functools

import jax
import jax.numpy as jnp
import ml_dtypes
import numpy as np
from jax import lax
from jax.experimental import pallas as pl
from jax.experimental.pallas import tpu as pltpu
from jax.sharding import PartitionSpec as P

SURF_ORDER = 6
NQ = 152
NCOEF = 456
RANK = 64
P_CAP = 128
LEAF_DEV = 64
BOX_DEV = 73
NROOT = 32
AXIS = "morton"
CHECK_RADIUS = 1.475
LEAF_UNROLL = 16

F32 = jnp.float32
BF16 = jnp.bfloat16


def surface_points():
    ticks = np.linspace(-1.0, 1.0, SURF_ORDER)
    last = SURF_ORDER - 1
    chosen = []
    for i in range(SURF_ORDER):
        for j in range(SURF_ORDER):
            for k in range(SURF_ORDER):
                if min(i, j, k) == 0 or max(i, j, k) == last:
                    chosen.append((ticks[i], ticks[j], ticks[k]))
    return CHECK_RADIUS * np.array(chosen).T


def direction_index():
    found = {}
    for u in range(-3, 4):
        for v in range(-3, 4):
            for w in range(-3, 4):
                if max(abs(u), abs(v), abs(w)) >= 2:
                    found[(u, v, w)] = len(found)
    return found


DIRS = direction_index()


def leaf_order():
    table = np.zeros((64, 64), np.float32)
    for leaf in range(64):
        x, y, z = leaf // 16, leaf // 4 % 4, leaf % 4
        octant = (x % 2) * 4 + (y % 2) * 2 + z % 2
        parent = (x // 2) * 4 + (y // 2) * 2 + z // 2
        table[leaf, octant * 8 + parent] = 1.0
    return table.astype(ml_dtypes.bfloat16)


def reachable(shift, target):
    return not (shift == -3 and target % 2 == 0) and not (shift == 3 and target % 2 == 1)


def cross_section_picks():
    table = np.zeros((4, 49 * 32, 128), np.float32)
    for place in range(4):
        y_bit, z_bit = place // 2, place % 2
        for pair in range(49):
            v, w = pair // 7 - 3, pair % 7 - 3
            for side, first, copies in ((4, 0, 1), (2, 16, 2)):
                for y in range(side):
                    for z in range(side):
                        if not (reachable(v, y) and reachable(w, z)):
                            continue
                        gy, gz = side * y_bit + y + v, side * z_bit + z + w
                        if not (0 <= gy < 2 * side and 0 <= gz < 2 * side):
                            continue
                        owner = (gy // side) * 2 + gz // side
                        source = (owner ^ place) * 32 + first + (gy % side) * side + gz % side
                        for copy in range(copies):
                            table[place, pair * 32 + first + 4 * copy + y * side + z, source] = 1.0
    return table.astype(ml_dtypes.bfloat16)


def device_level_table():
    rows = np.zeros((8, 24), np.int32)
    for place in range(8):
        parity, y_bit, z_bit = place // 4, place // 2 % 2, place % 2
        columns = (-2, 2, 3) if parity == 0 else (-2, -1, 3)
        for n, column in enumerate(columns):
            for other in range(4):
                entry = (column - parity, other // 2 - y_bit, other % 2 - z_bit)
                rows[place, n * 4 + other] = DIRS[entry]
            rows[place, 12 + n] = column
    return rows


def split(x):
    high = x.astype(BF16).astype(F32)
    return high, x - high


def stacked(x):
    high, low = split(x)
    return jnp.concatenate([high, low], axis=0).astype(BF16)


def dot(a, b):
    return jnp.dot(a, b, preferred_element_type=F32)


def dot_nt(a, b):
    return lax.dot_general(a, b, (((1,), (1,)), ((), ())), preferred_element_type=F32)


def product(x, w_high, w_low, dot=dot):
    rows = x.shape[0]
    both = stacked(x)
    top = dot(both, w_high)
    rest = dot(both, w_low)
    return top[:rows] + (top[rows:] + rest[:rows])


def upward_kernel(
    offsets_hbm, forces_hbm, counts_hbm, surface_hbm, points_hbm, order_hbm, uc2ue_hbm, m2m_hbm,
    compress_hbm, shared, block,
    offsets, forces, counts, surface, points, order, uc2ue, m2m, compress,
    m2m_high, m2m_low, check, sems,
):
    pairs = (
        (offsets_hbm, offsets), (forces_hbm, forces), (counts_hbm, counts), (surface_hbm, surface),
        (points_hbm, points), (order_hbm, order), (uc2ue_hbm, uc2ue), (compress_hbm, compress),
        (m2m_hbm, m2m),
    )
    fetches = [pltpu.make_async_copy(a, b, sems.at[n]) for n, (a, b) in enumerate(pairs)]
    for fetch in fetches:
        fetch.start()
    for fetch in fetches[:4]:
        fetch.wait()
    slots = lax.broadcasted_iota(jnp.int32, (1, P_CAP), 1)
    zero = jnp.zeros((1, P_CAP), F32)
    one = jnp.ones((1, P_CAP), F32)

    def leaf(l, carry):
        columns = pl.ds(pl.multiple_of(l * P_CAP, P_CAP), P_CAP)
        u = offsets[:, columns]
        live = (slots < counts[l]).astype(F32)
        f = forces[:, columns] * live
        r = [surface[s] - u[s : s + 1] for s in range(3)]
        inverse = lax.rsqrt(r[0] * r[0] + r[1] * r[1] + r[2] * r[2])
        along = r[0] * f[0:1] + r[1] * f[1:2] + r[2] * f[2:3]
        pulled = along * (inverse * inverse * inverse)
        both = jnp.concatenate([inverse, pulled], axis=1)
        high, low = split(both)
        left = jnp.concatenate(
            [jnp.concatenate([f, zero], axis=0), jnp.concatenate([-u, one], axis=0)], axis=1
        )
        left = stacked(left)
        top = dot_nt(left, high.astype(BF16))
        rest = dot_nt(left, low.astype(BF16))
        sums = top[0:4] + (top[4:8] + rest[0:4])
        octant = (l >> 4 & 1) * 4 + (l >> 2 & 1) * 2 + (l & 1)
        parent = (l >> 5 & 1) * 4 + (l >> 3 & 1) * 2 + (l >> 1 & 1)
        check[pl.ds(octant * 8 + parent, 1)] = sums[None]
        return carry

    lax.fori_loop(0, LEAF_DEV, leaf, 0, unroll=LEAF_UNROLL)

    for fetch in fetches[4:8]:
        fetch.wait()
    density = jnp.zeros((LEAF_DEV, NCOEF), F32)
    for s in range(3):
        rows = check[:, s, :] + check[:, 3, :] * points[s : s + 1, :]
        w_high, w_low = split(uc2ue[s * NQ : (s + 1) * NQ, :])
        density = density + product(rows, w_high.astype(BF16), w_low.astype(BF16))
    shrink = compress[...]
    shrink = jnp.concatenate([shrink, shrink], axis=0)
    s_high, s_low = split(shrink)
    s_high, s_low = s_high.astype(BF16), s_low.astype(BF16)
    lower = lax.broadcasted_iota(jnp.int32, (1, 128), 1) < RANK
    leaves = product(density, s_high, s_low, dot_nt).astype(BF16)
    leaves = dot(order[...], leaves)
    block[0:16, 0:128] = jnp.where(lower, leaves[0:16], leaves[16:32]).astype(BF16)
    block[0:16, 128:256] = jnp.where(lower, leaves[32:48], leaves[48:64]).astype(BF16)

    fetches[8].wait()
    parents = jnp.zeros((8, NCOEF), F32)
    for o in range(8):
        w_high, w_low = split(m2m[o])
        w_high, w_low = w_high.astype(BF16), w_low.astype(BF16)
        m2m_high[o] = w_high
        m2m_low[o] = w_low
        parents = parents + product(density[o * 8 : o * 8 + 8], w_high, w_low)
    middle = product(parents, s_high, s_low, dot_nt).astype(BF16).astype(F32)
    middle = jnp.where(lower, middle[0:4], middle[4:8])

    def one_row(x, w_high, w_low, dot=dot):
        high, low = split(x)
        row = lax.broadcasted_iota(jnp.int32, (8, 1), 0)
        both = jnp.where(row == 0, high, jnp.where(row == 1, low, 0.0)).astype(BF16)
        top = dot(both, w_high)
        rest = dot(both, w_low)
        return top[0:1] + (top[1:2] + rest[0:1])

    device = jnp.zeros((1, NCOEF), F32)
    for o in range(8):
        device = device + one_row(parents[o : o + 1], m2m_high[o], m2m_low[o])
    own = one_row(device, s_high, s_low, dot_nt).astype(BF16).astype(F32)
    octant = lax.axis_index(AXIS) % 8
    above = one_row(device, m2m_high[octant], m2m_low[octant])
    above = one_row(above, s_high, s_low, dot_nt)
    shared[...] = jnp.broadcast_to(jnp.where(lower, own, above), shared.shape)
    middle = jnp.concatenate([middle, jnp.zeros((12, 128), F32)], axis=0).astype(BF16)
    block[16:32, 0:128] = middle
    block[16:32, 128:256] = middle


def operators_kernel(source_hbm, out, source, turned, sem):
    fetch = pltpu.make_async_copy(source_hbm, source, sem)
    fetch.start()
    directions = source.shape[2]
    rows = (directions + 7) // 8 * 8
    pitch = turned.shape[1] // 16
    shape = (rows, directions)
    unit = lax.broadcasted_iota(jnp.int32, shape, 0) == lax.broadcasted_iota(jnp.int32, shape, 1)
    unit = unit.astype(F32).astype(BF16)
    fetch.wait()
    for g in range(16):
        four = jnp.concatenate([source[g + 16 * part] for part in range(4)], axis=0)
        moved = dot_nt(unit, four)
        for half in range(2):
            turned[half, g * pitch : g * pitch + rows, :] = moved[:, half * 128 : half * 128 + 128]
    for d in range(directions):
        parts = []
        for half in range(2):
            pair = turned[half, pl.ds(d, 16, stride=pitch), :]
            parts += [pair, pltpu.roll(pair, RANK, 1)]
        out[d] = jnp.concatenate(parts, axis=0)[:, :RANK].astype(BF16)


def far_kernel(table, own, below, above, picks_hbm, m2l, boxes, device_ops, picks, near, sem):
    me = lax.axis_index(AXIS)
    fetch = pltpu.make_async_copy(picks_hbm.at[me % 4], picks, sem)
    fetch.start()
    lower = lax.broadcasted_iota(jnp.int32, (1, 128), 1) < RANK
    for n in range(12):
        device_ops[n] = m2l[table[me % 8, n]]

    x01, x23, x45, x67 = below[...], own[:, 0:128], own[:, 128:256], above[...]

    def crossed(a, b):
        return jnp.where(lower, pltpu.roll(a, RANK, 1), pltpu.roll(b, RANK, 1))

    x01, x23, x45, x67 = (x.astype(F32) for x in (x01, x23, x45, x67))
    none = jnp.zeros_like(x01)
    blocks = [
        x01, x23, x45, x67,
        crossed(x01, x23), crossed(x23, x45), crossed(x45, x67),
        crossed(none, x01), crossed(none, x23), crossed(x45, none), crossed(x67, none),
    ]
    wide = jnp.concatenate(blocks, axis=1).astype(BF16)
    fetch.wait()
    near[...] = dot(picks[...], wide).astype(BF16)

    def part(pair, rows, which):
        if which is None:
            return jnp.zeros((16, 128), BF16)
        first = pair * 32 + rows
        return near[first : first + 16, which * 128 : which * 128 + 128]

    even = {0: (7, 4, 5, 9), 1: (8, 5, 6, 10)}
    odd = {0: (0, 1, 2, None), 1: (1, 2, 3, None)}
    even_far = {0: (7, 2), 1: (8, 3)}
    odd_far = {0: (0, 9), 1: (1, 10)}
    level1 = ((7, 4, 6, 10), (0, 1, 3, None))
    level1_far = ((7, 3), (0, 10))
    first_rows = lax.broadcasted_iota(jnp.int32, (16, 128), 0) < 4
    total = jnp.zeros((80, RANK), F32)
    for pair in range(49):
        v, w = pair // 7 - 3, pair % 7 - 3
        close = max(abs(v), abs(w)) < 2
        shifts = (-3, -2, 2, 3) if close else range(-3, 4)
        e, o, l1 = (even_far, odd_far, level1_far) if close else (even, odd, level1)
        rows = []
        for halves in (e, o):
            for a in range(2):
                rows.append(jnp.concatenate([part(pair, 0, k) for k in halves[a]], axis=1))
        both = [
            jnp.where(first_rows, part(pair, 16, a).astype(F32), part(pair, 16, b).astype(F32)).astype(BF16)
            for a, b in zip(*l1)
        ]
        rows.append(jnp.concatenate(both, axis=1))
        left = jnp.concatenate(rows, axis=0)
        operator = [m2l[DIRS[(u, v, w)]] for u in shifts]
        if not close:
            left = left[:, : 7 * RANK]
        total = total + dot(left, jnp.concatenate(operator, axis=0))
    boxes[...] = jnp.zeros(boxes.shape, F32)
    boxes[1:9, :] = total[64:72]
    for p in range(2):
        for a in range(2):
            x = 2 * a + p
            first = (p * 2 + a) * 16
            boxes[9 + 16 * x : 25 + 16 * x, :] = total[first : first + 16]


def top_kernel(table, partial, device_ops, shared, root_ops, boxes, roots, base, shifted, turned):
    me = lax.axis_index(AXIS)
    lower = lax.broadcasted_iota(jnp.int32, (1, 128), 1) < RANK
    gathered = shared[...]
    high_half = jnp.sum(gathered.reshape(NROOT, 8, 128), axis=1).astype(BF16).astype(F32)
    low_half = pltpu.roll(high_half, RANK, 1)
    base[...] = jnp.zeros(base.shape, F32)
    shifted[...] = jnp.zeros(shifted.shape, F32)
    base[32:64, :] = jnp.where(lower, low_half, 0.0)
    shifted[31:63, :] = jnp.where(lower, 0.0, high_half)
    base[...] = base[...] + shifted[...]
    total = jnp.zeros((NROOT, RANK), F32)
    for distance in range(-31, 32, 2):
        if distance == -1:
            continue
        source = base[32 + distance : 64 + distance, :]
        first = distance + NROOT - 1
        if distance == 1:
            source = jnp.where(lower, 0.0, source)
        if distance == 31:
            total = total + dot(source[:, :RANK].astype(BF16), root_ops[first])
            continue
        operator = jnp.concatenate([root_ops[first], root_ops[first + 1]], axis=0)
        total = total + dot(source.astype(BF16), operator)
    roots[...] = total

    first_column = me // 8 * 2
    columns_total = lax.axis_size(AXIS) // 4
    far = jnp.zeros((8, RANK), F32)
    for n in range(3):
        column = first_column + table[me % 8, 12 + n]
        inside = jnp.logical_and(column >= 0, column < columns_total)
        kept = jnp.where(inside, 1.0, 0.0).astype(F32)
        start = jnp.clip(column, 0, columns_total - 1) * 4
        for other in range(4):
            source = shared[pl.ds(start + other, 1), :][:, :RANK] * kept
            source = jnp.broadcast_to(source, (8, RANK)).astype(BF16)
            far = far + dot(source, device_ops[n * 4 + other])
    turned[...] = jnp.zeros(turned.shape, F32)
    turned[0:80, 0:RANK] = partial[...]
    turned[0:1, 0:RANK] = far[0:1]
    boxes[...] = turned[...].T[:RANK, :BOX_DEV]


def whole(space=pltpu.VMEM):
    return pl.BlockSpec(memory_space=space)


def upward(offsets, forces, counts, uc2ue, m2m_ops, compress):
    devices = lax.axis_size(AXIS)
    points = surface_points().astype(np.float32)
    spread = np.ascontiguousarray(np.broadcast_to(points[:, :, None], (3, NQ, P_CAP)))
    rows = np.zeros((8, NQ), np.float32)
    rows[:3] = points
    operands = (
        offsets, forces, counts, jnp.asarray(spread), jnp.asarray(rows), jnp.asarray(leaf_order()),
        uc2ue, m2m_ops, compress.T,
    )
    held = [pltpu.VMEM(x.shape, x.dtype) for x in operands]
    held[2] = pltpu.SMEM(counts.shape, counts.dtype)
    return pl.pallas_call(
        upward_kernel,
        out_shape=(
            jax.ShapeDtypeStruct((devices, 128), F32),
            jax.ShapeDtypeStruct((32, 256), BF16),
        ),
        in_specs=[whole(pltpu.HBM)] * len(operands),
        out_specs=(whole(), whole()),
        scratch_shapes=held
        + [
            pltpu.VMEM((8, NCOEF, NCOEF), BF16),
            pltpu.VMEM((8, NCOEF, NCOEF), BF16),
            pltpu.VMEM((LEAF_DEV, 4, NQ), F32),
            pltpu.SemaphoreType.DMA((len(operands),)),
        ],
        compiler_params=pltpu.CompilerParams(vmem_limit_bytes=58 * 2**20),
        name="upward",
    )(*operands)


def operators(m2l_ops):
    count = m2l_ops.shape[0]
    return pl.pallas_call(
        operators_kernel,
        out_shape=jax.ShapeDtypeStruct(m2l_ops.shape, BF16),
        in_specs=[whole(pltpu.HBM)],
        out_specs=whole(),
        scratch_shapes=[
            pltpu.VMEM((RANK, RANK, count), BF16),
            pltpu.VMEM((2, 16 * (count + 5), 128), F32),
            pltpu.SemaphoreType.DMA,
        ],
        compiler_params=pltpu.CompilerParams(vmem_limit_bytes=28 * 2**20),
        name="operators",
    )(jnp.transpose(m2l_ops, (1, 2, 0)))


def far_field(table, own, below, above, m2l):
    return pl.pallas_call(
        far_kernel,
        out_shape=(
            jax.ShapeDtypeStruct((80, RANK), F32),
            jax.ShapeDtypeStruct((12, RANK, RANK), BF16),
        ),
        in_specs=[whole(pltpu.SMEM), whole(), whole(), whole(), whole(pltpu.HBM), whole()],
        out_specs=(whole(), whole()),
        scratch_shapes=[
            pltpu.VMEM((49 * 32, 128), BF16),
            pltpu.VMEM((49 * 32, 11 * 128), BF16),
            pltpu.SemaphoreType.DMA,
        ],
        compiler_params=pltpu.CompilerParams(vmem_limit_bytes=28 * 2**20),
        name="far_field",
    )(table, own, below, above, jnp.asarray(cross_section_picks()), m2l)


def top_levels(table, partial, device_ops, shared, root_ops):
    boxes, roots = pl.pallas_call(
        top_kernel,
        out_shape=(
            jax.ShapeDtypeStruct((RANK, BOX_DEV), F32),
            jax.ShapeDtypeStruct((NROOT, RANK), F32),
        ),
        in_specs=[whole(pltpu.SMEM)] + [whole()] * 4,
        out_specs=(whole(), whole()),
        scratch_shapes=[
            pltpu.VMEM((96, 128), F32),
            pltpu.VMEM((96, 128), F32),
            pltpu.VMEM((128, 128), F32),
        ],
        compiler_params=pltpu.CompilerParams(vmem_limit_bytes=16 * 2**20),
        name="top_levels",
    )(table, partial, device_ops, shared, root_ops)
    return boxes.T, roots


def swapped(value, mask):
    devices = lax.axis_size(AXIS)
    return lax.ppermute(value, AXIS, [(s, s ^ mask) for s in range(devices)])


def swapped_columns(value):
    devices = lax.axis_size(AXIS)
    pairs = []
    for s in range(devices):
        column, place = divmod(s, 4)
        other = column + 1 if column % 2 == 1 else column - 1
        if 0 <= other < devices // 4:
            pairs.append((s, other * 4 + (place ^ 2)))
    return lax.ppermute(value, AXIS, pairs)


def body(offsets, forces, counts, uc2ue, m2m_ops, compress, m2l_ops, root_ops):
    me = lax.axis_index(AXIS)
    shared, block = upward(offsets, forces, counts, uc2ue, m2m_ops, compress)
    shared = lax.all_to_all(shared, AXIS, 0, 0, tiled=True)
    two = jnp.concatenate([block, swapped(block, 1)], axis=0)
    own = jnp.concatenate([two, swapped(two, 2)], axis=0)
    is_upper = me // 4 % 2 == 1
    low_side, high_side = own[:, :128], own[:, 128:]
    sibling = swapped(jnp.where(is_upper, low_side, high_side), 6)
    further = swapped_columns(jnp.where(is_upper, high_side, low_side))
    below = jnp.where(is_upper, sibling, further)
    above = jnp.where(is_upper, further, sibling)
    below = jnp.concatenate([below[64:], below[:64]], axis=0)
    above = jnp.concatenate([above[64:], above[:64]], axis=0)
    table = jnp.asarray(device_level_table())
    partial, device_ops = far_field(table, own, below, above, operators(m2l_ops))
    return top_levels(table, partial, device_ops, shared, root_ops)


def solution(mesh):
    placed = (P(None, AXIS), P(None, AXIS), P(AXIS), P(), P(), P(), P(), P())
    return jax.shard_map(
        body, mesh=mesh, in_specs=placed, out_specs=(P(AXIS, None), P()), check_vma=False
    )
```

```python
import functools

import jax
import jax.numpy as jnp
import ml_dtypes
import numpy as np
from jax import lax
from jax.experimental import pallas as pl
from jax.experimental.pallas import tpu as pltpu
from jax.sharding import PartitionSpec as P

SURF_ORDER = 6
NQ = 152
NCOEF = 456
RANK = 64
P_CAP = 128
LEAF_DEV = 64
BOX_DEV = 73
NROOT = 32
AXIS = "morton"
CHECK_RADIUS = 1.475
LEAF_UNROLL = 16

F32 = jnp.float32
BF16 = jnp.bfloat16


def surface_points():
    ticks = np.linspace(-1.0, 1.0, SURF_ORDER)
    last = SURF_ORDER - 1
    chosen = []
    for i in range(SURF_ORDER):
        for j in range(SURF_ORDER):
            for k in range(SURF_ORDER):
                if min(i, j, k) == 0 or max(i, j, k) == last:
                    chosen.append((ticks[i], ticks[j], ticks[k]))
    return CHECK_RADIUS * np.array(chosen).T


def direction_index():
    found = {}
    for u in range(-3, 4):
        for v in range(-3, 4):
            for w in range(-3, 4):
                if max(abs(u), abs(v), abs(w)) >= 2:
                    found[(u, v, w)] = len(found)
    return found


DIRS = direction_index()


def leaf_order():
    table = np.zeros((64, 64), np.float32)
    for leaf in range(64):
        x, y, z = leaf // 16, leaf // 4 % 4, leaf % 4
        octant = (x % 2) * 4 + (y % 2) * 2 + z % 2
        parent = (x // 2) * 4 + (y // 2) * 2 + z // 2
        table[leaf, octant * 8 + parent] = 1.0
    return table.astype(ml_dtypes.bfloat16)


def reachable(shift, target):
    return not (shift == -3 and target % 2 == 0) and not (shift == 3 and target % 2 == 1)


def cross_section_picks():
    table = np.zeros((4, 49 * 32, 128), np.float32)
    for place in range(4):
        y_bit, z_bit = place // 2, place % 2
        for pair in range(49):
            v, w = pair // 7 - 3, pair % 7 - 3
            for side, first, copies in ((4, 0, 1), (2, 16, 2)):
                for y in range(side):
                    for z in range(side):
                        if not (reachable(v, y) and reachable(w, z)):
                            continue
                        gy, gz = side * y_bit + y + v, side * z_bit + z + w
                        if not (0 <= gy < 2 * side and 0 <= gz < 2 * side):
                            continue
                        owner = (gy // side) * 2 + gz // side
                        source = (owner ^ place) * 32 + first + (gy % side) * side + gz % side
                        for copy in range(copies):
                            table[place, pair * 32 + first + 4 * copy + y * side + z, source] = 1.0
    return table.astype(ml_dtypes.bfloat16)


def device_level_table():
    rows = np.zeros((8, 24), np.int32)
    for place in range(8):
        parity, y_bit, z_bit = place // 4, place // 2 % 2, place % 2
        columns = (-2, 2, 3) if parity == 0 else (-2, -1, 3)
        for n, column in enumerate(columns):
            for other in range(4):
                entry = (column - parity, other // 2 - y_bit, other % 2 - z_bit)
                rows[place, n * 4 + other] = DIRS[entry]
            rows[place, 12 + n] = column
    return rows


def split(x):
    high = x.astype(BF16).astype(F32)
    return high, x - high


def stacked(x):
    high, low = split(x)
    return jnp.concatenate([high, low], axis=0).astype(BF16)


def dot(a, b):
    return jnp.dot(a, b, preferred_element_type=F32)


def dot_nt(a, b):
    return lax.dot_general(a, b, (((1,), (1,)), ((), ())), preferred_element_type=F32)


def product(x, w_high, w_low, dot=dot):
    rows = x.shape[0]
    both = stacked(x)
    top = dot(both, w_high)
    rest = dot(both, w_low)
    return top[:rows] + (top[rows:] + rest[:rows])


def upward_kernel(
    offsets_hbm, forces_hbm, counts_hbm, surface_hbm, points_hbm, order_hbm, uc2ue_hbm, m2m_hbm,
    compress_hbm, shared, block,
    offsets, forces, counts, surface, points, order, uc2ue, m2m, compress,
    m2m_high, m2m_low, check, sems,
):
    pairs = (
        (offsets_hbm, offsets), (forces_hbm, forces), (counts_hbm, counts), (surface_hbm, surface),
        (points_hbm, points), (order_hbm, order), (uc2ue_hbm, uc2ue), (compress_hbm, compress),
        (m2m_hbm, m2m),
    )
    fetches = [pltpu.make_async_copy(a, b, sems.at[n]) for n, (a, b) in enumerate(pairs)]
    for fetch in fetches:
        fetch.start()
    for fetch in fetches[:4]:
        fetch.wait()
    slots = lax.broadcasted_iota(jnp.int32, (1, P_CAP), 1)
    zero = jnp.zeros((1, P_CAP), F32)
    one = jnp.ones((1, P_CAP), F32)

    def leaf(l, carry):
        columns = pl.ds(pl.multiple_of(l * P_CAP, P_CAP), P_CAP)
        u = offsets[:, columns]
        live = (slots < counts[l]).astype(F32)
        f = forces[:, columns] * live
        r = [surface[s] - u[s : s + 1] for s in range(3)]
        inverse = lax.rsqrt(r[0] * r[0] + r[1] * r[1] + r[2] * r[2])
        along = r[0] * f[0:1] + r[1] * f[1:2] + r[2] * f[2:3]
        pulled = along * (inverse * inverse * inverse)
        both = jnp.concatenate([inverse, pulled], axis=1)
        high, low = split(both)
        left = jnp.concatenate(
            [jnp.concatenate([f, zero], axis=0), jnp.concatenate([-u, one], axis=0)], axis=1
        )
        left = stacked(left)
        top = dot_nt(left, high.astype(BF16))
        rest = dot_nt(left, low.astype(BF16))
        sums = top[0:4] + (top[4:8] + rest[0:4])
        octant = (l >> 4 & 1) * 4 + (l >> 2 & 1) * 2 + (l & 1)
        parent = (l >> 5 & 1) * 4 + (l >> 3 & 1) * 2 + (l >> 1 & 1)
        check[pl.ds(octant * 8 + parent, 1)] = sums[None]
        return carry

    lax.fori_loop(0, LEAF_DEV, leaf, 0, unroll=LEAF_UNROLL)

    for fetch in fetches[4:8]:
        fetch.wait()
    density = jnp.zeros((LEAF_DEV, NCOEF), F32)
    for s in range(3):
        rows = check[:, s, :] + check[:, 3, :] * points[s : s + 1, :]
        w_high, w_low = split(uc2ue[s * NQ : (s + 1) * NQ, :])
        density = density + product(rows, w_high.astype(BF16), w_low.astype(BF16))
    shrink = compress[...]
    shrink = jnp.concatenate([shrink, shrink], axis=0)
    s_high, s_low = split(shrink)
    s_high, s_low = s_high.astype(BF16), s_low.astype(BF16)
    lower = lax.broadcasted_iota(jnp.int32, (1, 128), 1) < RANK
    leaves = product(density, s_high, s_low, dot_nt).astype(BF16)
    leaves = dot(order[...], leaves)
    block[0:16, 0:128] = jnp.where(lower, leaves[0:16], leaves[16:32]).astype(BF16)
    block[0:16, 128:256] = jnp.where(lower, leaves[32:48], leaves[48:64]).astype(BF16)

    fetches[8].wait()
    parents = jnp.zeros((8, NCOEF), F32)
    for o in range(8):
        w_high, w_low = split(m2m[o])
        w_high, w_low = w_high.astype(BF16), w_low.astype(BF16)
        m2m_high[o] = w_high
        m2m_low[o] = w_low
        parents = parents + product(density[o * 8 : o * 8 + 8], w_high, w_low)
    middle = product(parents, s_high, s_low, dot_nt).astype(BF16).astype(F32)
    middle = jnp.where(lower, middle[0:4], middle[4:8])

    def one_row(x, w_high, w_low, dot=dot):
        high, low = split(x)
        row = lax.broadcasted_iota(jnp.int32, (8, 1), 0)
        both = jnp.where(row == 0, high, jnp.where(row == 1, low, 0.0)).astype(BF16)
        top = dot(both, w_high)
        rest = dot(both, w_low)
        return top[0:1] + (top[1:2] + rest[0:1])

    device = jnp.zeros((1, NCOEF), F32)
    for o in range(8):
        device = device + one_row(parents[o : o + 1], m2m_high[o], m2m_low[o])
    own = one_row(device, s_high, s_low, dot_nt).astype(BF16).astype(F32)
    octant = lax.axis_index(AXIS) % 8
    above = one_row(device, m2m_high[octant], m2m_low[octant])
    above = one_row(above, s_high, s_low, dot_nt)
    shared[...] = jnp.broadcast_to(jnp.where(lower, own, above), shared.shape)
    middle = jnp.concatenate([middle, jnp.zeros((12, 128), F32)], axis=0).astype(BF16)
    block[16:32, 0:128] = middle
    block[16:32, 128:256] = middle


def operators_kernel(source_hbm, out, source, turned, sem):
    fetch = pltpu.make_async_copy(source_hbm, source, sem)
    fetch.start()
    directions = source.shape[2]
    rows = (directions + 7) // 8 * 8
    pitch = turned.shape[1] // 16
    shape = (rows, directions)
    unit = lax.broadcasted_iota(jnp.int32, shape, 0) == lax.broadcasted_iota(jnp.int32, shape, 1)
    unit = unit.astype(F32).astype(BF16)
    fetch.wait()
    for g in range(16):
        four = jnp.concatenate([source[g + 16 * part] for part in range(4)], axis=0)
        moved = dot_nt(unit, four)
        for half in range(2):
            turned[half, g * pitch : g * pitch + rows, :] = moved[:, half * 128 : half * 128 + 128]
    for d in range(directions):
        parts = []
        for half in range(2):
            pair = turned[half, pl.ds(d, 16, stride=pitch), :]
            parts += [pair, pltpu.roll(pair, RANK, 1)]
        out[d] = jnp.concatenate(parts, axis=0)[:, :RANK].astype(BF16)


def far_kernel(table, own, below, above, picks_hbm, m2l, boxes, device_ops, picks, near, sem):
    me = lax.axis_index(AXIS)
    fetch = pltpu.make_async_copy(picks_hbm.at[me % 4], picks, sem)
    fetch.start()
    lower = lax.broadcasted_iota(jnp.int32, (1, 128), 1) < RANK
    for n in range(12):
        device_ops[n] = m2l[table[me % 8, n]]

    x01, x23, x45, x67 = below[...], own[:, 0:128], own[:, 128:256], above[...]

    def crossed(a, b):
        return jnp.where(lower, pltpu.roll(a, RANK, 1), pltpu.roll(b, RANK, 1))

    x01, x23, x45, x67 = (x.astype(F32) for x in (x01, x23, x45, x67))
    none = jnp.zeros_like(x01)
    blocks = [
        x01, x23, x45, x67,
        crossed(x01, x23), crossed(x23, x45), crossed(x45, x67),
        crossed(none, x01), crossed(none, x23), crossed(x45, none), crossed(x67, none),
    ]
    wide = jnp.concatenate(blocks, axis=1).astype(BF16)
    fetch.wait()
    near[...] = dot(picks[...], wide).astype(BF16)

    def part(pair, rows, which):
        if which is None:
            return jnp.zeros((16, 128), BF16)
        first = pair * 32 + rows
        return near[first : first + 16, which * 128 : which * 128 + 128]

    even = {0: (7, 4, 5, 9), 1: (8, 5, 6, 10)}
    odd = {0: (0, 1, 2, None), 1: (1, 2, 3, None)}
    even_far = {0: (7, 2), 1: (8, 3)}
    odd_far = {0: (0, 9), 1: (1, 10)}
    level1 = ((7, 4, 6, 10), (0, 1, 3, None))
    level1_far = ((7, 3), (0, 10))
    first_rows = lax.broadcasted_iota(jnp.int32, (16, 128), 0) < 4
    total = jnp.zeros((80, RANK), F32)
    for pair in range(49):
        v, w = pair // 7 - 3, pair % 7 - 3
        close = max(abs(v), abs(w)) < 2
        shifts = (-3, -2, 2, 3) if close else range(-3, 4)
        e, o, l1 = (even_far, odd_far, level1_far) if close else (even, odd, level1)
        rows = []
        for halves in (e, o):
            for a in range(2):
                rows.append(jnp.concatenate([part(pair, 0, k) for k in halves[a]], axis=1))
        both = [
            jnp.where(first_rows, part(pair, 16, a).astype(F32), part(pair, 16, b).astype(F32)).astype(BF16)
            for a, b in zip(*l1)
        ]
        rows.append(jnp.concatenate(both, axis=1))
        left = jnp.concatenate(rows, axis=0)
        operator = [m2l[DIRS[(u, v, w)]] for u in shifts]
        if not close:
            left = left[:, : 7 * RANK]
        total = total + dot(left, jnp.concatenate(operator, axis=0))
    boxes[...] = jnp.zeros(boxes.shape, F32)
    boxes[1:9, :] = total[64:72]
    for p in range(2):
        for a in range(2):
            x = 2 * a + p
            first = (p * 2 + a) * 16
            boxes[9 + 16 * x : 25 + 16 * x, :] = total[first : first + 16]


def top_kernel(table, partial, device_ops, shared, root_ops, boxes, roots, base, shifted, turned):
    me = lax.axis_index(AXIS)
    lower = lax.broadcasted_iota(jnp.int32, (1, 128), 1) < RANK
    gathered = shared[...]
    high_half = jnp.sum(gathered.reshape(NROOT, 8, 128), axis=1).astype(BF16).astype(F32)
    low_half = pltpu.roll(high_half, RANK, 1)
    base[...] = jnp.zeros(base.shape, F32)
    shifted[...] = jnp.zeros(shifted.shape, F32)
    base[32:64, :] = jnp.where(lower, low_half, 0.0)
    shifted[31:63, :] = jnp.where(lower, 0.0, high_half)
    base[...] = base[...] + shifted[...]
    total = jnp.zeros((NROOT, RANK), F32)
    for distance in range(-31, 32, 2):
        if distance == -1:
            continue
        source = base[32 + distance : 64 + distance, :]
        first = distance + NROOT - 1
        if distance == 1:
            source = jnp.where(lower, 0.0, source)
        if distance == 31:
            total = total + dot(source[:, :RANK].astype(BF16), root_ops[first])
            continue
        operator = jnp.concatenate([root_ops[first], root_ops[first + 1]], axis=0)
        total = total + dot(source.astype(BF16), operator)
    roots[...] = total

    first_column = me // 8 * 2
    columns_total = lax.axis_size(AXIS) // 4
    far = jnp.zeros((8, RANK), F32)
    for n in range(3):
        column = first_column + table[me % 8, 12 + n]
        inside = jnp.logical_and(column >= 0, column < columns_total)
        kept = jnp.where(inside, 1.0, 0.0).astype(F32)
        start = jnp.clip(column, 0, columns_total - 1) * 4
        for other in range(4):
            source = shared[pl.ds(start + other, 1), :][:, :RANK] * kept
            source = jnp.broadcast_to(source, (8, RANK)).astype(BF16)
            far = far + dot(source, device_ops[n * 4 + other])
    turned[...] = jnp.zeros(turned.shape, F32)
    turned[0:80, 0:RANK] = partial[...]
    turned[0:1, 0:RANK] = far[0:1]
    boxes[...] = turned[...].T[:RANK, :BOX_DEV]


def whole(space=pltpu.VMEM):
    return pl.BlockSpec(memory_space=space)


def upward(offsets, forces, counts, uc2ue, m2m_ops, compress):
    devices = lax.axis_size(AXIS)
    points = surface_points().astype(np.float32)
    spread = np.ascontiguousarray(np.broadcast_to(points[:, :, None], (3, NQ, P_CAP)))
    rows = np.zeros((8, NQ), np.float32)
    rows[:3] = points
    operands = (
        offsets, forces, counts, jnp.asarray(spread), jnp.asarray(rows), jnp.asarray(leaf_order()),
        uc2ue, m2m_ops, compress.T,
    )
    operands = tuple(pltpu.with_memory_space_constraint(x, pltpu.HBM) for x in operands)
    held = [pltpu.VMEM(x.shape, x.dtype) for x in operands]
    held[2] = pltpu.SMEM(counts.shape, counts.dtype)
    return pl.pallas_call(
        upward_kernel,
        out_shape=(
            pltpu.VMEM((devices, 128), F32),
            pltpu.VMEM((32, 256), BF16),
        ),
        in_specs=[whole(pltpu.HBM)] * len(operands),
        out_specs=(whole(), whole()),
        scratch_shapes=held
        + [
            pltpu.VMEM((8, NCOEF, NCOEF), BF16),
            pltpu.VMEM((8, NCOEF, NCOEF), BF16),
            pltpu.VMEM((LEAF_DEV, 4, NQ), F32),
            pltpu.SemaphoreType.DMA((len(operands),)),
        ],
        compiler_params=pltpu.CompilerParams(vmem_limit_bytes=40 * 2**20),
        name="upward",
    )(*operands)


def operators(m2l_ops):
    count = m2l_ops.shape[0]
    return pl.pallas_call(
        operators_kernel,
        out_shape=jax.ShapeDtypeStruct(m2l_ops.shape, BF16),
        in_specs=[whole(pltpu.HBM)],
        out_specs=whole(),
        scratch_shapes=[
            pltpu.VMEM((RANK, RANK, count), BF16),
            pltpu.VMEM((2, 16 * (count + 5), 128), F32),
            pltpu.SemaphoreType.DMA,
        ],
        compiler_params=pltpu.CompilerParams(vmem_limit_bytes=28 * 2**20),
        name="operators",
    )(jnp.transpose(m2l_ops, (1, 2, 0)))


def far_field(table, own, below, above, m2l):
    return pl.pallas_call(
        far_kernel,
        out_shape=(
            jax.ShapeDtypeStruct((80, RANK), F32),
            jax.ShapeDtypeStruct((12, RANK, RANK), BF16),
        ),
        in_specs=[whole(pltpu.SMEM), whole(), whole(), whole(), whole(pltpu.HBM), whole()],
        out_specs=(whole(), whole()),
        scratch_shapes=[
            pltpu.VMEM((49 * 32, 128), BF16),
            pltpu.VMEM((49 * 32, 11 * 128), BF16),
            pltpu.SemaphoreType.DMA,
        ],
        compiler_params=pltpu.CompilerParams(vmem_limit_bytes=28 * 2**20),
        name="far_field",
    )(table, own, below, above, jnp.asarray(cross_section_picks()), m2l)


def top_levels(table, partial, device_ops, shared, root_ops):
    boxes, roots = pl.pallas_call(
        top_kernel,
        out_shape=(
            jax.ShapeDtypeStruct((RANK, BOX_DEV), F32),
            jax.ShapeDtypeStruct((NROOT, RANK), F32),
        ),
        in_specs=[whole(pltpu.SMEM)] + [whole()] * 4,
        out_specs=(whole(), whole()),
        scratch_shapes=[
            pltpu.VMEM((96, 128), F32),
            pltpu.VMEM((96, 128), F32),
            pltpu.VMEM((128, 128), F32),
        ],
        compiler_params=pltpu.CompilerParams(vmem_limit_bytes=16 * 2**20),
        name="top_levels",
    )(table, partial, device_ops, shared, root_ops)
    return boxes.T, roots


def swapped(value, mask):
    devices = lax.axis_size(AXIS)
    return lax.ppermute(value, AXIS, [(s, s ^ mask) for s in range(devices)])


def swapped_columns(value):
    devices = lax.axis_size(AXIS)
    pairs = []
    for s in range(devices):
        column, place = divmod(s, 4)
        other = column + 1 if column % 2 == 1 else column - 1
        if 0 <= other < devices // 4:
            pairs.append((s, other * 4 + (place ^ 2)))
    return lax.ppermute(value, AXIS, pairs)


def body(offsets, forces, counts, uc2ue, m2m_ops, compress, m2l_ops, root_ops):
    me = lax.axis_index(AXIS)
    shared, block = upward(offsets, forces, counts, uc2ue, m2m_ops, compress)
    shared = lax.all_to_all(shared, AXIS, 0, 0, tiled=True)
    two = jnp.concatenate([block, swapped(block, 1)], axis=0)
    own = jnp.concatenate([two, swapped(two, 2)], axis=0)
    is_upper = me // 4 % 2 == 1
    low_side, high_side = own[:, :128], own[:, 128:]
    sibling = swapped(jnp.where(is_upper, low_side, high_side), 6)
    further = swapped_columns(jnp.where(is_upper, high_side, low_side))
    below = jnp.where(is_upper, sibling, further)
    above = jnp.where(is_upper, further, sibling)
    below = jnp.concatenate([below[64:], below[:64]], axis=0)
    above = jnp.concatenate([above[64:], above[:64]], axis=0)
    table = jnp.asarray(device_level_table())
    partial, device_ops = far_field(table, own, below, above, operators(m2l_ops))
    return top_levels(table, partial, device_ops, shared, root_ops)


def solution(mesh):
    placed = (P(None, AXIS), P(None, AXIS), P(AXIS), P(), P(), P(), P(), P())
    return jax.shard_map(
        body, mesh=mesh, in_specs=placed, out_specs=(P(AXIS, None), P()), check_vma=False
    )
```

```python
import functools

import jax
import jax.numpy as jnp
import ml_dtypes
import numpy as np
from jax import lax
from jax.experimental import pallas as pl
from jax.experimental.pallas import tpu as pltpu
from jax.sharding import PartitionSpec as P

SURF_ORDER = 6
NQ = 152
NCOEF = 456
RANK = 64
P_CAP = 128
LEAF_DEV = 64
BOX_DEV = 73
NROOT = 32
AXIS = "morton"
CHECK_RADIUS = 1.475
LEAF_UNROLL = 64

F32 = jnp.float32
BF16 = jnp.bfloat16


def surface_points():
    ticks = np.linspace(-1.0, 1.0, SURF_ORDER)
    last = SURF_ORDER - 1
    chosen = []
    for i in range(SURF_ORDER):
        for j in range(SURF_ORDER):
            for k in range(SURF_ORDER):
                if min(i, j, k) == 0 or max(i, j, k) == last:
                    chosen.append((ticks[i], ticks[j], ticks[k]))
    return CHECK_RADIUS * np.array(chosen).T


def direction_index():
    found = {}
    for u in range(-3, 4):
        for v in range(-3, 4):
            for w in range(-3, 4):
                if max(abs(u), abs(v), abs(w)) >= 2:
                    found[(u, v, w)] = len(found)
    return found


DIRS = direction_index()


def leaf_order():
    table = np.zeros((64, 64), np.float32)
    for leaf in range(64):
        x, y, z = leaf // 16, leaf // 4 % 4, leaf % 4
        octant = (x % 2) * 4 + (y % 2) * 2 + z % 2
        parent = (x // 2) * 4 + (y // 2) * 2 + z // 2
        table[leaf, octant * 8 + parent] = 1.0
    return table.astype(ml_dtypes.bfloat16)


def reachable(shift, target):
    return not (shift == -3 and target % 2 == 0) and not (shift == 3 and target % 2 == 1)


def cross_section_picks():
    table = np.zeros((4, 49 * 32, 128), np.float32)
    for place in range(4):
        y_bit, z_bit = place // 2, place % 2
        for pair in range(49):
            v, w = pair // 7 - 3, pair % 7 - 3
            for side, first, copies in ((4, 0, 1), (2, 16, 2)):
                for y in range(side):
                    for z in range(side):
                        if not (reachable(v, y) and reachable(w, z)):
                            continue
                        gy, gz = side * y_bit + y + v, side * z_bit + z + w
                        if not (0 <= gy < 2 * side and 0 <= gz < 2 * side):
                            continue
                        owner = (gy // side) * 2 + gz // side
                        source = (owner ^ place) * 32 + first + (gy % side) * side + gz % side
                        for copy in range(copies):
                            table[place, pair * 32 + first + 4 * copy + y * side + z, source] = 1.0
    return table.astype(ml_dtypes.bfloat16)


def device_level_table():
    rows = np.zeros((8, 24), np.int32)
    for place in range(8):
        parity, y_bit, z_bit = place // 4, place // 2 % 2, place % 2
        columns = (-2, 2, 3) if parity == 0 else (-2, -1, 3)
        for n, column in enumerate(columns):
            for other in range(4):
                entry = (column - parity, other // 2 - y_bit, other % 2 - z_bit)
                rows[place, n * 4 + other] = DIRS[entry]
            rows[place, 12 + n] = column
    return rows


def split(x):
    high = x.astype(BF16)
    return high, (x - high.astype(F32)).astype(BF16)


def stacked(x):
    high = x.astype(BF16).astype(F32)
    return jnp.concatenate([high, x - high], axis=0).astype(BF16)


def dot(a, b):
    return jnp.dot(a, b, preferred_element_type=F32)


def dot_nt(a, b):
    return lax.dot_general(a, b, (((1,), (1,)), ((), ())), preferred_element_type=F32)


def product(x, w_high, w_low, dot=dot):
    rows = x.shape[0]
    both = stacked(x)
    top = dot(both, w_high)
    rest = dot(both, w_low)
    return top[:rows] + (top[rows:] + rest[:rows])


def upward_kernel(
    offsets_hbm, forces_hbm, counts_hbm, surface_hbm, points_hbm, order_hbm, uc2ue_hbm, m2m_hbm,
    compress_hbm, shared, block,
    offsets, forces, counts, surface, points, order, uc2ue, m2m, compress,
    m2m_high, m2m_low, check, sems,
):
    pairs = (
        (offsets_hbm, offsets), (forces_hbm, forces), (counts_hbm, counts), (surface_hbm, surface),
        (points_hbm, points), (order_hbm, order), (uc2ue_hbm, uc2ue), (compress_hbm, compress),
        (m2m_hbm, m2m),
    )
    fetches = [pltpu.make_async_copy(a, b, sems.at[n]) for n, (a, b) in enumerate(pairs)]
    for fetch in fetches:
        fetch.start()
    for fetch in fetches[:4]:
        fetch.wait()
    slots = lax.broadcasted_iota(jnp.int32, (1, P_CAP), 1)
    zero = jnp.zeros((1, P_CAP), F32)
    one = jnp.ones((1, P_CAP), F32)

    def leaf(l, carry):
        columns = pl.ds(pl.multiple_of(l * P_CAP, P_CAP), P_CAP)
        u = offsets[:, columns]
        live = (slots < counts[l]).astype(F32)
        f = forces[:, columns] * live
        r = [surface[s] - u[s : s + 1] for s in range(3)]
        inverse = lax.rsqrt(r[0] * r[0] + r[1] * r[1] + r[2] * r[2])
        along = r[0] * f[0:1] + r[1] * f[1:2] + r[2] * f[2:3]
        pulled = along * (inverse * inverse * inverse)
        both = jnp.concatenate([inverse, pulled], axis=1)
        high, low = split(both)
        left = jnp.concatenate(
            [jnp.concatenate([f, zero], axis=0), jnp.concatenate([-u, one], axis=0)], axis=1
        )
        left = stacked(left)
        top = dot_nt(left, high)
        rest = dot_nt(left, low)
        sums = top[0:4] + (top[4:8] + rest[0:4])
        octant = (l >> 4 & 1) * 4 + (l >> 2 & 1) * 2 + (l & 1)
        parent = (l >> 5 & 1) * 4 + (l >> 3 & 1) * 2 + (l >> 1 & 1)
        check[pl.ds(octant * 8 + parent, 1)] = sums[None]
        return carry

    lax.fori_loop(0, LEAF_DEV, leaf, 0, unroll=LEAF_UNROLL)

    for fetch in fetches[4:8]:
        fetch.wait()
    density = jnp.zeros((LEAF_DEV, NCOEF), F32)
    for s in range(3):
        rows = check[:, s, :] + check[:, 3, :] * points[s : s + 1, :]
        w_high, w_low = split(uc2ue[s * NQ : (s + 1) * NQ, :])
        density = density + product(rows, w_high, w_low)
    shrink = compress[...]
    shrink = jnp.concatenate([shrink, shrink], axis=0)
    s_high, s_low = split(shrink)
    lower = lax.broadcasted_iota(jnp.int32, (1, 128), 1) < RANK
    leaves = product(density, s_high, s_low, dot_nt).astype(BF16)
    leaves = dot(order[...], leaves)
    block[0:16, 0:128] = jnp.where(lower, leaves[0:16], leaves[16:32]).astype(BF16)
    block[0:16, 128:256] = jnp.where(lower, leaves[32:48], leaves[48:64]).astype(BF16)

    fetches[8].wait()
    parents = jnp.zeros((8, NCOEF), F32)
    for o in range(8):
        w_high, w_low = split(m2m[o])
        m2m_high[o] = w_high
        m2m_low[o] = w_low
        parents = parents + product(density[o * 8 : o * 8 + 8], w_high, w_low)
    middle = product(parents, s_high, s_low, dot_nt).astype(BF16).astype(F32)
    middle = jnp.where(lower, middle[0:4], middle[4:8])

    def one_row(x, w_high, w_low, dot=dot):
        high, low = (part.astype(F32) for part in split(x))
        row = lax.broadcasted_iota(jnp.int32, (8, 1), 0)
        both = jnp.where(row == 0, high, jnp.where(row == 1, low, 0.0)).astype(BF16)
        top = dot(both, w_high)
        rest = dot(both, w_low)
        return top[0:1] + (top[1:2] + rest[0:1])

    device = jnp.zeros((1, NCOEF), F32)
    for o in range(8):
        device = device + one_row(parents[o : o + 1], m2m_high[o], m2m_low[o])
    own = one_row(device, s_high, s_low, dot_nt).astype(BF16).astype(F32)
    octant = lax.axis_index(AXIS) % 8
    above = one_row(device, m2m_high[octant], m2m_low[octant])
    above = one_row(above, s_high, s_low, dot_nt)
    shared[...] = jnp.broadcast_to(jnp.where(lower, own, above), shared.shape)
    middle = jnp.concatenate([middle, jnp.zeros((12, 128), F32)], axis=0).astype(BF16)
    block[16:32, 0:128] = middle
    block[16:32, 128:256] = middle


def operators_kernel(source_hbm, out_hbm, source, turned, out, sem, out_sems):
    fetch = pltpu.make_async_copy(source_hbm, source, sem)
    fetch.start()
    directions = source.shape[2]
    rows = (directions + 7) // 8 * 8
    pitch = turned.shape[1] // 16
    shape = (rows, directions)
    unit = lax.broadcasted_iota(jnp.int32, shape, 0) == lax.broadcasted_iota(jnp.int32, shape, 1)
    unit = unit.astype(F32).astype(BF16)
    fetch.wait()
    for g in range(16):
        four = jnp.concatenate([source[g + 16 * part] for part in range(4)], axis=0)
        moved = dot_nt(unit, four)
        for half in range(2):
            turned[half, g * pitch : g * pitch + rows, :] = moved[:, half * 128 : half * 128 + 128]
    part_size, all_leaving = (directions + 3) // 4, []
    for d in range(directions):
        parts = []
        for half in range(2):
            pair = turned[half, pl.ds(d, 16, stride=pitch), :]
            parts += [pair, pltpu.roll(pair, RANK, 1)]
        out[d] = jnp.concatenate(parts, axis=0)[:, :RANK].astype(BF16)
        if (d + 1) % part_size == 0 or d + 1 == directions:
            chunk = d // part_size
            first = chunk * part_size
            leaving = pltpu.make_async_copy(
                out.at[first : d + 1], out_hbm.at[first : d + 1], out_sems.at[chunk]
            )
            leaving.start()
            all_leaving.append(leaving)
    for leaving in all_leaving:
        leaving.wait()


def far_kernel(
    table, own, below, above, picks_hbm, m2l_hbm, root_hbm, boxes, device_ops, root_ops,
    picks, near, m2l, sem, m2l_sem, root_sem,
):
    me = lax.axis_index(AXIS)
    fetch = pltpu.make_async_copy(picks_hbm.at[me % 4], picks, sem)
    fetch.start()
    fetch_m2l = pltpu.make_async_copy(m2l_hbm, m2l, m2l_sem)
    fetch_m2l.start()
    fetch_root = pltpu.make_async_copy(root_hbm, root_ops, root_sem)
    fetch_root.start()
    lower = lax.broadcasted_iota(jnp.int32, (1, 128), 1) < RANK

    x01, x23, x45, x67 = below[...], own[:, 0:128], own[:, 128:256], above[...]

    def crossed(a, b):
        return jnp.where(lower, pltpu.roll(a, RANK, 1), pltpu.roll(b, RANK, 1))

    x01, x23, x45, x67 = (x.astype(F32) for x in (x01, x23, x45, x67))
    none = jnp.zeros_like(x01)
    blocks = [
        x01, x23, x45, x67,
        crossed(x01, x23), crossed(x23, x45), crossed(x45, x67),
        crossed(none, x01), crossed(none, x23), crossed(x45, none), crossed(x67, none),
    ]
    wide = jnp.concatenate(blocks, axis=1).astype(BF16)
    fetch.wait()
    near[...] = dot(picks[...], wide).astype(BF16)

    def part(pair, rows, which):
        if which is None:
            return jnp.zeros((16, 128), BF16)
        first = pair * 32 + rows
        return near[first : first + 16, which * 128 : which * 128 + 128]

    even = {0: (7, 4, 5, 9), 1: (8, 5, 6, 10)}
    odd = {0: (0, 1, 2, None), 1: (1, 2, 3, None)}
    even_far = {0: (7, 2), 1: (8, 3)}
    odd_far = {0: (0, 9), 1: (1, 10)}
    level1 = ((7, 4, 6, 10), (0, 1, 3, None))
    level1_far = ((7, 3), (0, 10))
    first_rows = lax.broadcasted_iota(jnp.int32, (16, 128), 0) < 4
    total = jnp.zeros((80, RANK), F32)
    fetch_m2l.wait()
    for n in range(12):
        device_ops[n] = m2l[table[me % 8, n]]
    for pair in range(49):
        v, w = pair // 7 - 3, pair % 7 - 3
        close = max(abs(v), abs(w)) < 2
        shifts = (-3, -2, 2, 3) if close else range(-3, 4)
        e, o, l1 = (even_far, odd_far, level1_far) if close else (even, odd, level1)
        rows = []
        for halves in (e, o):
            for a in range(2):
                rows.append(jnp.concatenate([part(pair, 0, k) for k in halves[a]], axis=1))
        both = [
            jnp.where(first_rows, part(pair, 16, a).astype(F32), part(pair, 16, b).astype(F32)).astype(BF16)
            for a, b in zip(*l1)
        ]
        rows.append(jnp.concatenate(both, axis=1))
        left = jnp.concatenate(rows, axis=0)
        operator = [m2l[DIRS[(u, v, w)]] for u in shifts]
        if not close:
            left = left[:, : 7 * RANK]
        total = total + dot(left, jnp.concatenate(operator, axis=0))
    fetch_root.wait()
    boxes[...] = jnp.zeros(boxes.shape, F32)
    boxes[1:9, :] = total[64:72]
    for p in range(2):
        for a in range(2):
            x = 2 * a + p
            first = (p * 2 + a) * 16
            boxes[9 + 16 * x : 25 + 16 * x, :] = total[first : first + 16]


def top_kernel(table, partial, device_ops, shared, root_ops, boxes, roots, base, shifted, turned):
    me = lax.axis_index(AXIS)
    lower = lax.broadcasted_iota(jnp.int32, (1, 128), 1) < RANK
    gathered = shared[...]
    high_half = jnp.sum(gathered.reshape(NROOT, 8, 128), axis=1).astype(BF16).astype(F32)
    low_half = pltpu.roll(high_half, RANK, 1)
    base[...] = jnp.zeros(base.shape, F32)
    shifted[...] = jnp.zeros(shifted.shape, F32)
    base[32:64, :] = jnp.where(lower, low_half, 0.0)
    shifted[31:63, :] = jnp.where(lower, 0.0, high_half)
    base[...] = base[...] + shifted[...]
    total = jnp.zeros((NROOT, RANK), F32)
    for distance in range(-31, 32, 2):
        if distance == -1:
            continue
        source = base[32 + distance : 64 + distance, :]
        first = distance + NROOT - 1
        if distance == 1:
            source = jnp.where(lower, 0.0, source)
        if distance == 31:
            total = total + dot(source[:, :RANK].astype(BF16), root_ops[first])
            continue
        operator = jnp.concatenate([root_ops[first], root_ops[first + 1]], axis=0)
        total = total + dot(source.astype(BF16), operator)
    roots[...] = total

    first_column = me // 8 * 2
    columns_total = lax.axis_size(AXIS) // 4
    far = jnp.zeros((8, RANK), F32)
    for n in range(3):
        column = first_column + table[me % 8, 12 + n]
        inside = jnp.logical_and(column >= 0, column < columns_total)
        kept = jnp.where(inside, 1.0, 0.0).astype(F32)
        start = jnp.clip(column, 0, columns_total - 1) * 4
        for other in range(4):
            source = shared[pl.ds(start + other, 1), :][:, :RANK] * kept
            source = jnp.broadcast_to(source, (8, RANK)).astype(BF16)
            far = far + dot(source, device_ops[n * 4 + other])
    turned[...] = jnp.zeros(turned.shape, F32)
    turned[0:80, 0:RANK] = partial[...]
    turned[0:1, 0:RANK] = far[0:1]
    boxes[...] = turned[...].T[:RANK, :BOX_DEV]


def whole(space=pltpu.VMEM):
    return pl.BlockSpec(memory_space=space)


def upward(offsets, forces, counts, uc2ue, m2m_ops, compress):
    devices = lax.axis_size(AXIS)
    points = surface_points().astype(np.float32)
    spread = np.ascontiguousarray(np.broadcast_to(points[:, :, None], (3, NQ, P_CAP)))
    rows = np.zeros((8, NQ), np.float32)
    rows[:3] = points
    operands = (
        offsets, forces, counts, jnp.asarray(spread), jnp.asarray(rows), jnp.asarray(leaf_order()),
        uc2ue, m2m_ops, compress.T,
    )
    operands = tuple(pltpu.with_memory_space_constraint(x, pltpu.HBM) for x in operands)
    held = [pltpu.VMEM(x.shape, x.dtype) for x in operands]
    held[2] = pltpu.SMEM(counts.shape, counts.dtype)
    return pl.pallas_call(
        upward_kernel,
        out_shape=(
            pltpu.VMEM((devices, 128), F32),
            pltpu.VMEM((32, 256), BF16),
        ),
        in_specs=[whole(pltpu.HBM)] * len(operands),
        out_specs=(whole(), whole()),
        scratch_shapes=held
        + [
            pltpu.VMEM((8, NCOEF, NCOEF), BF16),
            pltpu.VMEM((8, NCOEF, NCOEF), BF16),
            pltpu.VMEM((LEAF_DEV, 4, NQ), F32),
            pltpu.SemaphoreType.DMA((len(operands),)),
        ],
        compiler_params=pltpu.CompilerParams(vmem_limit_bytes=40 * 2**20),
        name="upward",
    )(*operands)


def operators(m2l_ops):
    count = m2l_ops.shape[0]
    return pl.pallas_call(
        operators_kernel,
        out_shape=pltpu.HBM(m2l_ops.shape, BF16),
        in_specs=[whole(pltpu.HBM)],
        out_specs=whole(pltpu.HBM),
        scratch_shapes=[
            pltpu.VMEM((RANK, RANK, count), BF16),
            pltpu.VMEM((2, 16 * (count + 5), 128), F32),
            pltpu.VMEM(m2l_ops.shape, BF16),
            pltpu.SemaphoreType.DMA,
            pltpu.SemaphoreType.DMA((4,)),
        ],
        compiler_params=pltpu.CompilerParams(vmem_limit_bytes=28 * 2**20),
        name="operators",
    )(jnp.transpose(m2l_ops, (1, 2, 0)))


def far_field(table, own, below, above, m2l, root_ops):
    held = (jnp.asarray(cross_section_picks()), m2l, root_ops)
    held = [pltpu.with_memory_space_constraint(x, pltpu.HBM) for x in held]
    return pl.pallas_call(
        far_kernel,
        out_shape=(
            jax.ShapeDtypeStruct((80, RANK), F32),
            jax.ShapeDtypeStruct((12, RANK, RANK), BF16),
            jax.ShapeDtypeStruct(root_ops.shape, BF16),
        ),
        in_specs=[whole(pltpu.SMEM), whole(), whole(), whole()] + [whole(pltpu.HBM)] * 3,
        out_specs=(whole(),) * 3,
        scratch_shapes=[
            pltpu.VMEM((49 * 32, 128), BF16),
            pltpu.VMEM((49 * 32, 11 * 128), BF16),
            pltpu.VMEM(m2l.shape, BF16),
            pltpu.SemaphoreType.DMA,
            pltpu.SemaphoreType.DMA,
            pltpu.SemaphoreType.DMA,
        ],
        compiler_params=pltpu.CompilerParams(vmem_limit_bytes=28 * 2**20),
        name="far_field",
    )(table, own, below, above, *held)


def top_levels(table, partial, device_ops, shared, root_ops):
    boxes, roots = pl.pallas_call(
        top_kernel,
        out_shape=(
            jax.ShapeDtypeStruct((RANK, BOX_DEV), F32),
            jax.ShapeDtypeStruct((NROOT, RANK), F32),
        ),
        in_specs=[whole(pltpu.SMEM)] + [whole()] * 4,
        out_specs=(whole(), whole()),
        scratch_shapes=[
            pltpu.VMEM((96, 128), F32),
            pltpu.VMEM((96, 128), F32),
            pltpu.VMEM((128, 128), F32),
        ],
        compiler_params=pltpu.CompilerParams(vmem_limit_bytes=16 * 2**20),
        name="top_levels",
    )(table, partial, device_ops, shared, root_ops)
    return boxes.T, roots


def swapped(value, mask):
    devices = lax.axis_size(AXIS)
    return lax.ppermute(value, AXIS, [(s, s ^ mask) for s in range(devices)])


def swapped_columns(value):
    devices = lax.axis_size(AXIS)
    pairs = []
    for s in range(devices):
        column, place = divmod(s, 4)
        other = column + 1 if column % 2 == 1 else column - 1
        if 0 <= other < devices // 4:
            pairs.append((s, other * 4 + (place ^ 2)))
    return lax.ppermute(value, AXIS, pairs)


def body(offsets, forces, counts, uc2ue, m2m_ops, compress, m2l_ops, root_ops):
    me = lax.axis_index(AXIS)
    shared, block = upward(offsets, forces, counts, uc2ue, m2m_ops, compress)
    shared = lax.all_to_all(shared, AXIS, 0, 0, tiled=True)
    two = jnp.concatenate([block, swapped(block, 1)], axis=0)
    own = jnp.concatenate([two, swapped(two, 2)], axis=0)
    own, m2l = lax.optimization_barrier((own, operators(m2l_ops)))
    is_upper = me // 4 % 2 == 1
    low_side, high_side = own[:, :128], own[:, 128:]
    sibling = swapped(jnp.where(is_upper, low_side, high_side), 6)
    further = swapped_columns(jnp.where(is_upper, high_side, low_side))
    below = jnp.where(is_upper, sibling, further)
    above = jnp.where(is_upper, further, sibling)
    below = jnp.concatenate([below[64:], below[:64]], axis=0)
    above = jnp.concatenate([above[64:], above[:64]], axis=0)
    table = jnp.asarray(device_level_table())
    partial, device_ops, root_ops = far_field(table, own, below, above, m2l, root_ops)
    return top_levels(table, partial, device_ops, shared, root_ops)


def solution(mesh):
    placed = (P(None, AXIS), P(None, AXIS), P(AXIS), P(), P(), P(), P(), P())
    return jax.shard_map(
        body, mesh=mesh, in_specs=placed, out_specs=(P(AXIS, None), P()), check_vma=False
    )
```

```python
import functools

import jax
import jax.numpy as jnp
import ml_dtypes
import numpy as np
from jax import lax
from jax.experimental import pallas as pl
from jax.experimental.pallas import tpu as pltpu
from jax.sharding import PartitionSpec as P

SURF_ORDER = 6
NQ = 152
NCOEF = 456
RANK = 64
P_CAP = 128
LEAF_DEV = 64
BOX_DEV = 73
NROOT = 32
AXIS = "morton"
CHECK_RADIUS = 1.475
LEAF_UNROLL = 64

F32 = jnp.float32
BF16 = jnp.bfloat16


def surface_points():
    ticks = np.linspace(-1.0, 1.0, SURF_ORDER)
    last = SURF_ORDER - 1
    chosen = []
    for i in range(SURF_ORDER):
        for j in range(SURF_ORDER):
            for k in range(SURF_ORDER):
                if min(i, j, k) == 0 or max(i, j, k) == last:
                    chosen.append((ticks[i], ticks[j], ticks[k]))
    return CHECK_RADIUS * np.array(chosen).T


def direction_index():
    found = {}
    for u in range(-3, 4):
        for v in range(-3, 4):
            for w in range(-3, 4):
                if max(abs(u), abs(v), abs(w)) >= 2:
                    found[(u, v, w)] = len(found)
    return found


DIRS = direction_index()


def leaf_order():
    table = np.zeros((64, 64), np.float32)
    for leaf in range(64):
        x, y, z = leaf // 16, leaf // 4 % 4, leaf % 4
        octant = (x % 2) * 4 + (y % 2) * 2 + z % 2
        parent = (x // 2) * 4 + (y // 2) * 2 + z // 2
        table[leaf, octant * 8 + parent] = 1.0
    return table.astype(ml_dtypes.bfloat16)


def reachable(shift, target):
    return not (shift == -3 and target % 2 == 0) and not (shift == 3 and target % 2 == 1)


def cross_section_picks():
    table = np.zeros((4, 49 * 32, 128), np.float32)
    for place in range(4):
        y_bit, z_bit = place // 2, place % 2
        for pair in range(49):
            v, w = pair // 7 - 3, pair % 7 - 3
            for side, first, copies in ((4, 0, 1), (2, 16, 2)):
                for y in range(side):
                    for z in range(side):
                        if not (reachable(v, y) and reachable(w, z)):
                            continue
                        gy, gz = side * y_bit + y + v, side * z_bit + z + w
                        if not (0 <= gy < 2 * side and 0 <= gz < 2 * side):
                            continue
                        owner = (gy // side) * 2 + gz // side
                        source = (owner ^ place) * 32 + first + (gy % side) * side + gz % side
                        for copy in range(copies):
                            table[place, pair * 32 + first + 4 * copy + y * side + z, source] = 1.0
    return table.astype(ml_dtypes.bfloat16)


def device_level_table():
    rows = np.zeros((8, 24), np.int32)
    for place in range(8):
        parity, y_bit, z_bit = place // 4, place // 2 % 2, place % 2
        columns = (-2, 2, 3) if parity == 0 else (-2, -1, 3)
        for n, column in enumerate(columns):
            for other in range(4):
                entry = (column - parity, other // 2 - y_bit, other % 2 - z_bit)
                rows[place, n * 4 + other] = DIRS[entry]
            rows[place, 12 + n] = column
    return rows


def split(x):
    high = x.astype(BF16)
    return high, (x - high.astype(F32)).astype(BF16)


def stacked(x):
    high = x.astype(BF16).astype(F32)
    return jnp.concatenate([high, x - high], axis=0).astype(BF16)


def dot(a, b):
    return jnp.dot(a, b, preferred_element_type=F32)


def dot_nt(a, b):
    return lax.dot_general(a, b, (((1,), (1,)), ((), ())), preferred_element_type=F32)


def product(x, w_high, w_low, dot=dot):
    rows = x.shape[0]
    both = stacked(x)
    top = dot(both, w_high)
    rest = dot(both, w_low)
    return top[:rows] + (top[rows:] + rest[:rows])


def upward_kernel(
    offsets_hbm, forces_hbm, counts_hbm, surface_hbm, points_hbm, order_hbm, uc2ue_hbm, m2m_hbm,
    compress_hbm, shared, block,
    offsets, forces, counts, surface, points, order, uc2ue, m2m, compress,
    m2m_high, m2m_low, check, sems,
):
    pairs = (
        (offsets_hbm, offsets), (forces_hbm, forces), (counts_hbm, counts), (surface_hbm, surface),
        (points_hbm, points), (order_hbm, order), (uc2ue_hbm, uc2ue), (compress_hbm, compress),
        (m2m_hbm, m2m),
    )
    fetches = [pltpu.make_async_copy(a, b, sems.at[n]) for n, (a, b) in enumerate(pairs)]
    for fetch in fetches:
        fetch.start()
    for fetch in fetches[:4]:
        fetch.wait()
    slots = lax.broadcasted_iota(jnp.int32, (1, P_CAP), 1)
    zero = jnp.zeros((1, P_CAP), F32)
    one = jnp.ones((1, P_CAP), F32)

    def leaf(l, carry):
        columns = pl.ds(pl.multiple_of(l * P_CAP, P_CAP), P_CAP)
        u = offsets[:, columns]
        live = (slots < counts[l]).astype(F32)
        f = forces[:, columns] * live
        r = [surface[s] - u[s : s + 1] for s in range(3)]
        inverse = lax.rsqrt(r[0] * r[0] + r[1] * r[1] + r[2] * r[2])
        along = r[0] * f[0:1] + r[1] * f[1:2] + r[2] * f[2:3]
        pulled = along * (inverse * inverse * inverse)
        both = jnp.concatenate([inverse, pulled], axis=1)
        high, low = split(both)
        left = jnp.concatenate(
            [jnp.concatenate([f, zero], axis=0), jnp.concatenate([-u, one], axis=0)], axis=1
        )
        left = stacked(left)
        top = dot_nt(left, high)
        rest = dot_nt(left, low)
        sums = top[0:4] + (top[4:8] + rest[0:4])
        octant = (l >> 4 & 1) * 4 + (l >> 2 & 1) * 2 + (l & 1)
        parent = (l >> 5 & 1) * 4 + (l >> 3 & 1) * 2 + (l >> 1 & 1)
        check[pl.ds(octant * 8 + parent, 1)] = sums[None]
        return carry

    lax.fori_loop(0, LEAF_DEV, leaf, 0, unroll=LEAF_UNROLL)

    for fetch in fetches[4:8]:
        fetch.wait()
    density = jnp.zeros((LEAF_DEV, NCOEF), F32)
    for s in range(3):
        rows = check[:, s, :] + check[:, 3, :] * points[s : s + 1, :]
        w_high, w_low = split(uc2ue[s * NQ : (s + 1) * NQ, :])
        density = density + product(rows, w_high, w_low)
    shrink = compress[...]
    shrink = jnp.concatenate([shrink, shrink], axis=0)
    s_high, s_low = split(shrink)
    lower = lax.broadcasted_iota(jnp.int32, (1, 128), 1) < RANK
    leaves = product(density, s_high, s_low, dot_nt).astype(BF16)
    leaves = dot(order[...], leaves)
    block[0:16, 0:128] = jnp.where(lower, leaves[0:16], leaves[16:32]).astype(BF16)
    block[0:16, 128:256] = jnp.where(lower, leaves[32:48], leaves[48:64]).astype(BF16)

    fetches[8].wait()
    parents = jnp.zeros((8, NCOEF), F32)
    for o in range(8):
        w_high, w_low = split(m2m[o])
        m2m_high[o] = w_high
        m2m_low[o] = w_low
        parents = parents + product(density[o * 8 : o * 8 + 8], w_high, w_low)
    middle = product(parents, s_high, s_low, dot_nt).astype(BF16).astype(F32)
    middle = jnp.where(lower, middle[0:4], middle[4:8])

    def one_row(x, w_high, w_low, dot=dot):
        high, low = (part.astype(F32) for part in split(x))
        row = lax.broadcasted_iota(jnp.int32, (8, 1), 0)
        both = jnp.where(row == 0, high, jnp.where(row == 1, low, 0.0)).astype(BF16)
        top = dot(both, w_high)
        rest = dot(both, w_low)
        return top[0:1] + (top[1:2] + rest[0:1])

    device = jnp.zeros((1, NCOEF), F32)
    for o in range(8):
        device = device + one_row(parents[o : o + 1], m2m_high[o], m2m_low[o])
    own = one_row(device, s_high, s_low, dot_nt).astype(BF16).astype(F32)
    octant = lax.axis_index(AXIS) % 8
    above = one_row(device, m2m_high[octant], m2m_low[octant])
    above = one_row(above, s_high, s_low, dot_nt)
    shared[...] = jnp.broadcast_to(jnp.where(lower, own, above), shared.shape)
    middle = jnp.concatenate([middle, jnp.zeros((12, 128), F32)], axis=0).astype(BF16)
    block[16:32, 0:128] = middle
    block[16:32, 128:256] = middle


def operators_kernel(source_hbm, out_hbm, source, turned, out, sem, out_sems):
    fetch = pltpu.make_async_copy(source_hbm, source, sem)
    fetch.start()
    directions = source.shape[2]
    rows = (directions + 7) // 8 * 8
    pitch = turned.shape[1] // 16
    shape = (rows, directions)
    unit = lax.broadcasted_iota(jnp.int32, shape, 0) == lax.broadcasted_iota(jnp.int32, shape, 1)
    unit = unit.astype(F32).astype(BF16)
    fetch.wait()
    for g in range(16):
        four = jnp.concatenate([source[g + 16 * part] for part in range(4)], axis=0)
        moved = dot_nt(unit, four)
        for half in range(2):
            turned[half, g * pitch : g * pitch + rows, :] = moved[:, half * 128 : half * 128 + 128]
    lower = lax.broadcasted_iota(jnp.int32, (1, 128), 1) < RANK
    count = directions // 2
    part_size, all_leaving = (count + 3) // 4, []
    for d in range(count):
        parts = []
        for half in range(2):
            first = turned[half, pl.ds(d, 16, stride=pitch), :]
            second = turned[half, pl.ds(d + count, 16, stride=pitch), :]
            parts.append(jnp.where(lower, first, pltpu.roll(second, RANK, 1)))
            parts.append(jnp.where(lower, pltpu.roll(first, RANK, 1), second))
        out[d] = jnp.concatenate(parts, axis=0).astype(BF16)
        if (d + 1) % part_size == 0 or d + 1 == count:
            chunk = d // part_size
            start = chunk * part_size
            leaving = pltpu.make_async_copy(
                out.at[start : d + 1], out_hbm.at[start : d + 1], out_sems.at[chunk]
            )
            leaving.start()
            all_leaving.append(leaving)
    for leaving in all_leaving:
        leaving.wait()


def far_kernel(
    table, own, below, above, picks_hbm, m2l_hbm, root_hbm, boxes, device_ops, root_ops,
    picks, near, m2l, sem, m2l_sem, root_sem,
):
    me = lax.axis_index(AXIS)
    fetch = pltpu.make_async_copy(picks_hbm.at[me % 4], picks, sem)
    fetch.start()
    fetch_m2l = pltpu.make_async_copy(m2l_hbm, m2l, m2l_sem)
    fetch_m2l.start()
    fetch_root = pltpu.make_async_copy(root_hbm, root_ops, root_sem)
    fetch_root.start()
    lower = lax.broadcasted_iota(jnp.int32, (1, 128), 1) < RANK

    x01, x23, x45, x67 = below[...], own[:, 0:128], own[:, 128:256], above[...]

    def crossed(a, b):
        return jnp.where(lower, pltpu.roll(a, RANK, 1), pltpu.roll(b, RANK, 1))

    x01, x23, x45, x67 = (x.astype(F32) for x in (x01, x23, x45, x67))
    none = jnp.zeros_like(x01)
    blocks = [
        x01, x23, x45, x67,
        crossed(x01, x23), crossed(x23, x45), crossed(x45, x67),
        crossed(none, x01), crossed(none, x23), crossed(x45, none), crossed(x67, none),
    ]
    wide = jnp.concatenate(blocks, axis=1).astype(BF16)
    fetch.wait()
    near[...] = dot(picks[...], wide).astype(BF16)

    def part(pair, rows, which):
        if which is None:
            return jnp.zeros((16, 128), BF16)
        first = pair * 32 + rows
        return near[first : first + 16, which * 128 : which * 128 + 128]

    even = {0: (7, 4, 5, 9), 1: (8, 5, 6, 10)}
    odd = {0: (0, 1, 2, None), 1: (1, 2, 3, None)}
    even_far = {0: (7, 2), 1: (8, 3)}
    odd_far = {0: (0, 9), 1: (1, 10)}
    level1 = ((7, 4, 6, 10), (0, 1, 3, None))
    level1_far = ((7, 3), (0, 10))
    first_rows = lax.broadcasted_iota(jnp.int32, (16, 128), 0) < 4
    total = jnp.zeros((80, RANK), F32)
    fetch_m2l.wait()
    half_count = m2l.shape[0]
    for n in range(12):
        entry = table[me % 8, n]
        beside = entry >= half_count
        both = m2l[entry - jnp.where(beside, half_count, 0)].astype(F32)
        both = jnp.where(beside, pltpu.roll(both, RANK, 1), both)
        device_ops[n] = both[:, :RANK].astype(BF16)

    def operator_of(entry):
        lane = entry // half_count * RANK
        return m2l[entry % half_count, :, lane : lane + RANK]

    for pair in range(49):
        v, w = pair // 7 - 3, pair % 7 - 3
        close = max(abs(v), abs(w)) < 2
        shifts = (-3, -2, 2, 3) if close else range(-3, 4)
        e, o, l1 = (even_far, odd_far, level1_far) if close else (even, odd, level1)
        rows = []
        for halves in (e, o):
            for a in range(2):
                rows.append(jnp.concatenate([part(pair, 0, k) for k in halves[a]], axis=1))
        both = [
            jnp.where(first_rows, part(pair, 16, a).astype(F32), part(pair, 16, b).astype(F32)).astype(BF16)
            for a, b in zip(*l1)
        ]
        rows.append(jnp.concatenate(both, axis=1))
        left = jnp.concatenate(rows, axis=0)
        operator = [operator_of(DIRS[(u, v, w)]) for u in shifts]
        if not close:
            left = left[:, : 7 * RANK]
        total = total + dot(left, jnp.concatenate(operator, axis=0))
    fetch_root.wait()
    boxes[...] = jnp.zeros(boxes.shape, F32)
    boxes[1:9, :] = total[64:72]
    for p in range(2):
        for a in range(2):
            x = 2 * a + p
            first = (p * 2 + a) * 16
            boxes[9 + 16 * x : 25 + 16 * x, :] = total[first : first + 16]


def top_kernel(table, partial, device_ops, shared, root_ops, boxes, roots, base, shifted, turned):
    me = lax.axis_index(AXIS)
    lower = lax.broadcasted_iota(jnp.int32, (1, 128), 1) < RANK
    gathered = shared[...]
    high_half = jnp.sum(gathered.reshape(NROOT, 8, 128), axis=1).astype(BF16).astype(F32)
    low_half = pltpu.roll(high_half, RANK, 1)
    base[...] = jnp.zeros(base.shape, F32)
    shifted[...] = jnp.zeros(shifted.shape, F32)
    base[32:64, :] = jnp.where(lower, low_half, 0.0)
    shifted[31:63, :] = jnp.where(lower, 0.0, high_half)
    base[...] = base[...] + shifted[...]
    total = jnp.zeros((NROOT, RANK), F32)
    for distance in range(-31, 32, 2):
        if distance == -1:
            continue
        source = base[32 + distance : 64 + distance, :]
        first = distance + NROOT - 1
        if distance == 1:
            source = jnp.where(lower, 0.0, source)
        if distance == 31:
            total = total + dot(source[:, :RANK].astype(BF16), root_ops[first])
            continue
        operator = jnp.concatenate([root_ops[first], root_ops[first + 1]], axis=0)
        total = total + dot(source.astype(BF16), operator)
    roots[...] = total

    first_column = me // 8 * 2
    columns_total = lax.axis_size(AXIS) // 4
    far = jnp.zeros((8, RANK), F32)
    for n in range(3):
        column = first_column + table[me % 8, 12 + n]
        inside = jnp.logical_and(column >= 0, column < columns_total)
        kept = jnp.where(inside, 1.0, 0.0).astype(F32)
        start = jnp.clip(column, 0, columns_total - 1) * 4
        for other in range(4):
            source = shared[pl.ds(start + other, 1), :][:, :RANK] * kept
            source = jnp.broadcast_to(source, (8, RANK)).astype(BF16)
            far = far + dot(source, device_ops[n * 4 + other])
    turned[...] = jnp.zeros(turned.shape, F32)
    turned[0:80, 0:RANK] = partial[...]
    turned[0:1, 0:RANK] = far[0:1]
    boxes[...] = turned[...].T[:RANK, :BOX_DEV]


def whole(space=pltpu.VMEM):
    return pl.BlockSpec(memory_space=space)


def upward(offsets, forces, counts, uc2ue, m2m_ops, compress):
    devices = lax.axis_size(AXIS)
    points = surface_points().astype(np.float32)
    spread = np.ascontiguousarray(np.broadcast_to(points[:, :, None], (3, NQ, P_CAP)))
    rows = np.zeros((8, NQ), np.float32)
    rows[:3] = points
    operands = (
        offsets, forces, counts, jnp.asarray(spread), jnp.asarray(rows), jnp.asarray(leaf_order()),
        uc2ue, m2m_ops, compress.T,
    )
    operands = tuple(pltpu.with_memory_space_constraint(x, pltpu.HBM) for x in operands)
    held = [pltpu.VMEM(x.shape, x.dtype) for x in operands]
    held[2] = pltpu.SMEM(counts.shape, counts.dtype)
    return pl.pallas_call(
        upward_kernel,
        out_shape=(
            pltpu.VMEM((devices, 128), F32),
            pltpu.VMEM((32, 256), BF16),
        ),
        in_specs=[whole(pltpu.HBM)] * len(operands),
        out_specs=(whole(), whole()),
        scratch_shapes=held
        + [
            pltpu.VMEM((8, NCOEF, NCOEF), BF16),
            pltpu.VMEM((8, NCOEF, NCOEF), BF16),
            pltpu.VMEM((LEAF_DEV, 4, NQ), F32),
            pltpu.SemaphoreType.DMA((len(operands),)),
        ],
        compiler_params=pltpu.CompilerParams(vmem_limit_bytes=40 * 2**20),
        name="upward",
    )(*operands)


def operators(m2l_ops):
    count = m2l_ops.shape[0]
    return pl.pallas_call(
        operators_kernel,
        out_shape=pltpu.HBM((count // 2, RANK, 2 * RANK), BF16),
        in_specs=[whole(pltpu.HBM)],
        out_specs=whole(pltpu.HBM),
        scratch_shapes=[
            pltpu.VMEM((RANK, RANK, count), BF16),
            pltpu.VMEM((2, 16 * (count + 5), 128), F32),
            pltpu.VMEM((count // 2, RANK, 2 * RANK), BF16),
            pltpu.SemaphoreType.DMA,
            pltpu.SemaphoreType.DMA((4,)),
        ],
        compiler_params=pltpu.CompilerParams(vmem_limit_bytes=28 * 2**20),
        name="operators",
    )(jnp.transpose(m2l_ops, (1, 2, 0)))


def far_field(table, own, below, above, m2l, root_ops):
    held = (jnp.asarray(cross_section_picks()), m2l, root_ops)
    held = [pltpu.with_memory_space_constraint(x, pltpu.HBM) for x in held]
    return pl.pallas_call(
        far_kernel,
        out_shape=(
            jax.ShapeDtypeStruct((80, RANK), F32),
            jax.ShapeDtypeStruct((12, RANK, RANK), BF16),
            jax.ShapeDtypeStruct(root_ops.shape, BF16),
        ),
        in_specs=[whole(pltpu.SMEM), whole(), whole(), whole()] + [whole(pltpu.HBM)] * 3,
        out_specs=(whole(),) * 3,
        scratch_shapes=[
            pltpu.VMEM((49 * 32, 128), BF16),
            pltpu.VMEM((49 * 32, 11 * 128), BF16),
            pltpu.VMEM(m2l.shape, BF16),
            pltpu.SemaphoreType.DMA,
            pltpu.SemaphoreType.DMA,
            pltpu.SemaphoreType.DMA,
        ],
        compiler_params=pltpu.CompilerParams(vmem_limit_bytes=28 * 2**20),
        name="far_field",
    )(table, own, below, above, *held)


def top_levels(table, partial, device_ops, shared, root_ops):
    boxes, roots = pl.pallas_call(
        top_kernel,
        out_shape=(
            jax.ShapeDtypeStruct((RANK, BOX_DEV), F32),
            jax.ShapeDtypeStruct((NROOT, RANK), F32),
        ),
        in_specs=[whole(pltpu.SMEM)] + [whole()] * 4,
        out_specs=(whole(), whole()),
        scratch_shapes=[
            pltpu.VMEM((96, 128), F32),
            pltpu.VMEM((96, 128), F32),
            pltpu.VMEM((128, 128), F32),
        ],
        compiler_params=pltpu.CompilerParams(vmem_limit_bytes=16 * 2**20),
        name="top_levels",
    )(table, partial, device_ops, shared, root_ops)
    return boxes.T, roots


def swapped(value, mask):
    devices = lax.axis_size(AXIS)
    return lax.ppermute(value, AXIS, [(s, s ^ mask) for s in range(devices)])


def swapped_columns(value):
    devices = lax.axis_size(AXIS)
    pairs = []
    for s in range(devices):
        column, place = divmod(s, 4)
        other = column + 1 if column % 2 == 1 else column - 1
        if 0 <= other < devices // 4:
            pairs.append((s, other * 4 + (place ^ 2)))
    return lax.ppermute(value, AXIS, pairs)


def body(offsets, forces, counts, uc2ue, m2m_ops, compress, m2l_ops, root_ops):
    me = lax.axis_index(AXIS)
    shared, block = upward(offsets, forces, counts, uc2ue, m2m_ops, compress)
    shared = lax.all_to_all(shared, AXIS, 0, 0, tiled=True)
    two = jnp.concatenate([block, swapped(block, 1)], axis=0)
    own = jnp.concatenate([two, swapped(two, 2)], axis=0)
    own, m2l = lax.optimization_barrier((own, operators(m2l_ops)))
    is_upper = me // 4 % 2 == 1
    low_side, high_side = own[:, :128], own[:, 128:]
    sibling = swapped(jnp.where(is_upper, low_side, high_side), 6)
    further = swapped_columns(jnp.where(is_upper, high_side, low_side))
    below = jnp.where(is_upper, sibling, further)
    above = jnp.where(is_upper, further, sibling)
    below = jnp.concatenate([below[64:], below[:64]], axis=0)
    above = jnp.concatenate([above[64:], above[:64]], axis=0)
    table = jnp.asarray(device_level_table())
    partial, device_ops, root_ops = far_field(table, own, below, above, m2l, root_ops)
    return top_levels(table, partial, device_ops, shared, root_ops)


def solution(mesh):
    placed = (P(None, AXIS), P(None, AXIS), P(AXIS), P(), P(), P(), P(), P())
    return jax.shard_map(
        body, mesh=mesh, in_specs=placed, out_specs=(P(AXIS, None), P()), check_vma=False
    )
```

```python
import functools

import jax
import jax.numpy as jnp
import ml_dtypes
import numpy as np
from jax import lax
from jax.experimental import pallas as pl
from jax.experimental.pallas import tpu as pltpu
from jax.sharding import PartitionSpec as P

SURF_ORDER = 6
NQ = 152
NCOEF = 456
RANK = 64
P_CAP = 128
LEAF_DEV = 64
BOX_DEV = 73
NROOT = 32
AXIS = "morton"
CHECK_RADIUS = 1.475
LEAF_UNROLL = 64

F32 = jnp.float32
BF16 = jnp.bfloat16


def surface_points():
    ticks = np.linspace(-1.0, 1.0, SURF_ORDER)
    last = SURF_ORDER - 1
    chosen = []
    for i in range(SURF_ORDER):
        for j in range(SURF_ORDER):
            for k in range(SURF_ORDER):
                if min(i, j, k) == 0 or max(i, j, k) == last:
                    chosen.append((ticks[i], ticks[j], ticks[k]))
    return CHECK_RADIUS * np.array(chosen).T


def direction_index():
    found = {}
    for u in range(-3, 4):
        for v in range(-3, 4):
            for w in range(-3, 4):
                if max(abs(u), abs(v), abs(w)) >= 2:
                    found[(u, v, w)] = len(found)
    return found


DIRS = direction_index()


def leaf_order():
    table = np.zeros((64, 64), np.float32)
    for leaf in range(64):
        x, y, z = leaf // 16, leaf // 4 % 4, leaf % 4
        octant = (x % 2) * 4 + (y % 2) * 2 + z % 2
        parent = (x // 2) * 4 + (y // 2) * 2 + z // 2
        table[leaf, octant * 8 + parent] = 1.0
    return table.astype(ml_dtypes.bfloat16)


def reachable(shift, target):
    return not (shift == -3 and target % 2 == 0) and not (shift == 3 and target % 2 == 1)


def cross_section_picks():
    table = np.zeros((4, 49 * 32, 128), np.float32)
    for place in range(4):
        y_bit, z_bit = place // 2, place % 2
        for pair in range(49):
            v, w = pair // 7 - 3, pair % 7 - 3
            for side, first, copies in ((4, 0, 1), (2, 16, 2)):
                for y in range(side):
                    for z in range(side):
                        if not (reachable(v, y) and reachable(w, z)):
                            continue
                        gy, gz = side * y_bit + y + v, side * z_bit + z + w
                        if not (0 <= gy < 2 * side and 0 <= gz < 2 * side):
                            continue
                        owner = (gy // side) * 2 + gz // side
                        source = (owner ^ place) * 32 + first + (gy % side) * side + gz % side
                        for copy in range(copies):
                            table[place, pair * 32 + first + 4 * copy + y * side + z, source] = 1.0
    return table.astype(ml_dtypes.bfloat16)


def device_level_table():
    rows = np.zeros((8, 24), np.int32)
    for place in range(8):
        parity, y_bit, z_bit = place // 4, place // 2 % 2, place % 2
        columns = (-2, 2, 3) if parity == 0 else (-2, -1, 3)
        for n, column in enumerate(columns):
            for other in range(4):
                entry = (column - parity, other // 2 - y_bit, other % 2 - z_bit)
                rows[place, n * 4 + other] = DIRS[entry]
            rows[place, 12 + n] = column
    return rows


def split(x):
    high = x.astype(BF16)
    return high, (x - high.astype(F32)).astype(BF16)


def stacked(x):
    high = x.astype(BF16).astype(F32)
    return jnp.concatenate([high, x - high], axis=0).astype(BF16)


def dot(a, b):
    return jnp.dot(a, b, preferred_element_type=F32)


def dot_nt(a, b):
    return lax.dot_general(a, b, (((1,), (1,)), ((), ())), preferred_element_type=F32)


def product(x, w_high, w_low, dot=dot):
    rows = x.shape[0]
    both = stacked(x)
    top = dot(both, w_high)
    rest = dot(both, w_low)
    return top[:rows] + (top[rows:] + rest[:rows])


def upward_kernel(
    offsets_hbm, forces_hbm, counts_hbm, surface_hbm, points_hbm, order_hbm, uc2ue_hbm, m2m_hbm,
    compress_hbm, shared, block,
    offsets, forces, counts, surface, points, order, uc2ue, m2m, compress,
    m2m_high, m2m_low, check, sems,
):
    pairs = (
        (offsets_hbm, offsets), (forces_hbm, forces), (counts_hbm, counts), (surface_hbm, surface),
        (points_hbm, points), (order_hbm, order), (uc2ue_hbm, uc2ue), (compress_hbm, compress),
        (m2m_hbm, m2m),
    )
    fetches = [pltpu.make_async_copy(a, b, sems.at[n]) for n, (a, b) in enumerate(pairs)]
    for fetch in fetches:
        fetch.start()
    for fetch in fetches[:4]:
        fetch.wait()
    slots = lax.broadcasted_iota(jnp.int32, (1, P_CAP), 1)
    zero = jnp.zeros((1, P_CAP), F32)
    one = jnp.ones((1, P_CAP), F32)

    def leaf(l, carry):
        columns = pl.ds(pl.multiple_of(l * P_CAP, P_CAP), P_CAP)
        u = offsets[:, columns]
        live = (slots < counts[l]).astype(F32)
        f = forces[:, columns] * live
        r = [surface[s] - u[s : s + 1] for s in range(3)]
        inverse = lax.rsqrt(r[0] * r[0] + r[1] * r[1] + r[2] * r[2])
        along = r[0] * f[0:1] + r[1] * f[1:2] + r[2] * f[2:3]
        pulled = along * (inverse * inverse * inverse)
        both = jnp.concatenate([inverse, pulled], axis=1)
        high, low = split(both)
        left = jnp.concatenate(
            [jnp.concatenate([f, zero], axis=0), jnp.concatenate([-u, one], axis=0)], axis=1
        )
        left = stacked(left)
        top = dot_nt(left, high)
        rest = dot_nt(left, low)
        sums = top[0:4] + (top[4:8] + rest[0:4])
        octant = (l >> 4 & 1) * 4 + (l >> 2 & 1) * 2 + (l & 1)
        parent = (l >> 5 & 1) * 4 + (l >> 3 & 1) * 2 + (l >> 1 & 1)
        check[pl.ds(octant * 8 + parent, 1)] = sums[None]
        return carry

    lax.fori_loop(0, LEAF_DEV, leaf, 0, unroll=LEAF_UNROLL)

    for fetch in fetches[4:8]:
        fetch.wait()
    density = jnp.zeros((LEAF_DEV, NCOEF), F32)
    for s in range(3):
        rows = check[:, s, :] + check[:, 3, :] * points[s : s + 1, :]
        w_high, w_low = split(uc2ue[s * NQ : (s + 1) * NQ, :])
        density = density + product(rows, w_high, w_low)
    shrink = compress[...]
    shrink = jnp.concatenate([shrink, shrink], axis=0)
    s_high, s_low = split(shrink)
    lower = lax.broadcasted_iota(jnp.int32, (1, 128), 1) < RANK
    leaves = product(density, s_high, s_low, dot_nt).astype(BF16)
    leaves = dot(order[...], leaves)
    block[0:16, 0:128] = jnp.where(lower, leaves[0:16], leaves[16:32]).astype(BF16)
    block[0:16, 128:256] = jnp.where(lower, leaves[32:48], leaves[48:64]).astype(BF16)

    fetches[8].wait()
    parents = jnp.zeros((8, NCOEF), F32)
    for o in range(8):
        w_high, w_low = split(m2m[o])
        m2m_high[o] = w_high
        m2m_low[o] = w_low
        parents = parents + product(density[o * 8 : o * 8 + 8], w_high, w_low)
    middle = product(parents, s_high, s_low, dot_nt).astype(BF16).astype(F32)
    middle = jnp.where(lower, middle[0:4], middle[4:8])

    def one_row(x, w_high, w_low, dot=dot):
        high, low = (part.astype(F32) for part in split(x))
        row = lax.broadcasted_iota(jnp.int32, (8, 1), 0)
        both = jnp.where(row == 0, high, jnp.where(row == 1, low, 0.0)).astype(BF16)
        top = dot(both, w_high)
        rest = dot(both, w_low)
        return top[0:1] + (top[1:2] + rest[0:1])

    device = jnp.zeros((1, NCOEF), F32)
    for o in range(8):
        device = device + one_row(parents[o : o + 1], m2m_high[o], m2m_low[o])
    own = one_row(device, s_high, s_low, dot_nt).astype(BF16).astype(F32)
    octant = lax.axis_index(AXIS) % 8
    above = one_row(device, m2m_high[octant], m2m_low[octant])
    above = one_row(above, s_high, s_low, dot_nt)
    shared[...] = jnp.broadcast_to(jnp.where(lower, own, above), shared.shape)
    middle = jnp.concatenate([middle, jnp.zeros((12, 128), F32)], axis=0).astype(BF16)
    block[16:32, 0:128] = middle
    block[16:32, 128:256] = middle


def operators_kernel(source_hbm, out, source, turned, sem):
    fetch = pltpu.make_async_copy(source_hbm, source, sem)
    fetch.start()
    directions = source.shape[2]
    rows = (directions + 7) // 8 * 8
    pitch = turned.shape[1] // 16
    shape = (rows, directions)
    unit = lax.broadcasted_iota(jnp.int32, shape, 0) == lax.broadcasted_iota(jnp.int32, shape, 1)
    unit = unit.astype(F32).astype(BF16)
    fetch.wait()
    for g in range(16):
        four = jnp.concatenate([source[g + 16 * part] for part in range(4)], axis=0)
        moved = dot_nt(unit, four)
        for half in range(2):
            turned[half, g * pitch : g * pitch + rows, :] = moved[:, half * 128 : half * 128 + 128]
    lower = lax.broadcasted_iota(jnp.int32, (1, 128), 1) < RANK
    count = directions // 2
    for d in range(count):
        parts = []
        for half in range(2):
            first = turned[half, pl.ds(d, 16, stride=pitch), :]
            second = turned[half, pl.ds(d + count, 16, stride=pitch), :]
            parts.append(jnp.where(lower, first, pltpu.roll(second, RANK, 1)))
            parts.append(jnp.where(lower, pltpu.roll(first, RANK, 1), second))
        out[d] = jnp.concatenate(parts, axis=0).astype(BF16)


def far_kernel(
    table, own, below, above, m2l, picks_hbm, boxes, device_ops, picks, near, sem
):
    me = lax.axis_index(AXIS)
    fetch = pltpu.make_async_copy(picks_hbm.at[me % 4], picks, sem)
    fetch.start()
    lower = lax.broadcasted_iota(jnp.int32, (1, 128), 1) < RANK

    x01, x23, x45, x67 = below[...], own[:, 0:128], own[:, 128:256], above[...]

    def crossed(a, b):
        return jnp.where(lower, pltpu.roll(a, RANK, 1), pltpu.roll(b, RANK, 1))

    x01, x23, x45, x67 = (x.astype(F32) for x in (x01, x23, x45, x67))
    none = jnp.zeros_like(x01)
    blocks = [
        x01, x23, x45, x67,
        crossed(x01, x23), crossed(x23, x45), crossed(x45, x67),
        crossed(none, x01), crossed(none, x23), crossed(x45, none), crossed(x67, none),
    ]
    wide = jnp.concatenate(blocks, axis=1).astype(BF16)
    fetch.wait()
    near[...] = dot(picks[...], wide).astype(BF16)

    def part(pair, rows, which):
        if which is None:
            return jnp.zeros((16, 128), BF16)
        first = pair * 32 + rows
        return near[first : first + 16, which * 128 : which * 128 + 128]

    even = {0: (7, 4, 5, 9), 1: (8, 5, 6, 10)}
    odd = {0: (0, 1, 2, None), 1: (1, 2, 3, None)}
    even_far = {0: (7, 2), 1: (8, 3)}
    odd_far = {0: (0, 9), 1: (1, 10)}
    level1 = ((7, 4, 6, 10), (0, 1, 3, None))
    level1_far = ((7, 3), (0, 10))
    first_rows = lax.broadcasted_iota(jnp.int32, (16, 128), 0) < 4
    total = jnp.zeros((80, RANK), F32)
    half_count = m2l.shape[0]
    for n in range(12):
        entry = table[me % 8, n]
        beside = entry >= half_count
        both = m2l[entry - jnp.where(beside, half_count, 0)].astype(F32)
        both = jnp.where(beside, pltpu.roll(both, RANK, 1), both)
        device_ops[n] = both[:, :RANK].astype(BF16)

    def operator_of(entry):
        lane = entry // half_count * RANK
        return m2l[entry % half_count, :, lane : lane + RANK]

    for pair in range(49):
        v, w = pair // 7 - 3, pair % 7 - 3
        close = max(abs(v), abs(w)) < 2
        shifts = (-3, -2, 2, 3) if close else range(-3, 4)
        e, o, l1 = (even_far, odd_far, level1_far) if close else (even, odd, level1)
        rows = []
        for halves in (e, o):
            for a in range(2):
                rows.append(jnp.concatenate([part(pair, 0, k) for k in halves[a]], axis=1))
        both = [
            jnp.where(first_rows, part(pair, 16, a).astype(F32), part(pair, 16, b).astype(F32)).astype(BF16)
            for a, b in zip(*l1)
        ]
        rows.append(jnp.concatenate(both, axis=1))
        left = jnp.concatenate(rows, axis=0)
        operator = [operator_of(DIRS[(u, v, w)]) for u in shifts]
        if not close:
            left = left[:, : 7 * RANK]
        total = total + dot(left, jnp.concatenate(operator, axis=0))
    boxes[...] = jnp.zeros(boxes.shape, F32)
    boxes[1:9, :] = total[64:72]
    for p in range(2):
        for a in range(2):
            x = 2 * a + p
            first = (p * 2 + a) * 16
            boxes[9 + 16 * x : 25 + 16 * x, :] = total[first : first + 16]


def top_kernel(
    table, partial, device_ops, shared, root_hbm, boxes, roots, base, shifted, turned, root_ops, sem
):
    fetch = pltpu.make_async_copy(root_hbm, root_ops, sem)
    fetch.start()
    me = lax.axis_index(AXIS)
    lower = lax.broadcasted_iota(jnp.int32, (1, 128), 1) < RANK
    gathered = shared[...]
    high_half = jnp.sum(gathered.reshape(NROOT, 8, 128), axis=1).astype(BF16).astype(F32)
    low_half = pltpu.roll(high_half, RANK, 1)
    base[...] = jnp.zeros(base.shape, F32)
    shifted[...] = jnp.zeros(shifted.shape, F32)
    base[32:64, :] = jnp.where(lower, low_half, 0.0)
    shifted[31:63, :] = jnp.where(lower, 0.0, high_half)
    base[...] = base[...] + shifted[...]
    first_column = me // 8 * 2
    columns_total = lax.axis_size(AXIS) // 4
    far = jnp.zeros((8, RANK), F32)
    for n in range(3):
        column = first_column + table[me % 8, 12 + n]
        inside = jnp.logical_and(column >= 0, column < columns_total)
        kept = jnp.where(inside, 1.0, 0.0).astype(F32)
        start = jnp.clip(column, 0, columns_total - 1) * 4
        for other in range(4):
            source = shared[pl.ds(start + other, 1), :][:, :RANK] * kept
            source = jnp.broadcast_to(source, (8, RANK)).astype(BF16)
            far = far + dot(source, device_ops[n * 4 + other])
    turned[...] = jnp.zeros(turned.shape, F32)
    turned[0:80, 0:RANK] = partial[...]
    turned[0:1, 0:RANK] = far[0:1]
    boxes[...] = turned[...].T[:RANK, :BOX_DEV]

    fetch.wait()
    total = jnp.zeros((NROOT, RANK), F32)
    for distance in range(-31, 32, 2):
        if distance == -1:
            continue
        source = base[32 + distance : 64 + distance, :]
        first = distance + NROOT - 1
        if distance == 1:
            source = jnp.where(lower, 0.0, source)
        if distance == 31:
            total = total + dot(source[:, :RANK].astype(BF16), root_ops[first])
            continue
        operator = jnp.concatenate([root_ops[first], root_ops[first + 1]], axis=0)
        total = total + dot(source.astype(BF16), operator)
    roots[...] = total


def whole(space=pltpu.VMEM):
    return pl.BlockSpec(memory_space=space)


def upward(offsets, forces, counts, uc2ue, m2m_ops, compress):
    devices = lax.axis_size(AXIS)
    points = surface_points().astype(np.float32)
    spread = np.ascontiguousarray(np.broadcast_to(points[:, :, None], (3, NQ, P_CAP)))
    rows = np.zeros((8, NQ), np.float32)
    rows[:3] = points
    operands = (
        offsets, forces, counts, jnp.asarray(spread), jnp.asarray(rows), jnp.asarray(leaf_order()),
        uc2ue, m2m_ops, compress.T,
    )
    operands = tuple(pltpu.with_memory_space_constraint(x, pltpu.HBM) for x in operands)
    held = [pltpu.VMEM(x.shape, x.dtype) for x in operands]
    held[2] = pltpu.SMEM(counts.shape, counts.dtype)
    return pl.pallas_call(
        upward_kernel,
        out_shape=(
            pltpu.VMEM((devices, 128), F32),
            pltpu.VMEM((32, 256), BF16),
        ),
        in_specs=[whole(pltpu.HBM)] * len(operands),
        out_specs=(whole(), whole()),
        scratch_shapes=held
        + [
            pltpu.VMEM((8, NCOEF, NCOEF), BF16),
            pltpu.VMEM((8, NCOEF, NCOEF), BF16),
            pltpu.VMEM((LEAF_DEV, 4, NQ), F32),
            pltpu.SemaphoreType.DMA((len(operands),)),
        ],
        compiler_params=pltpu.CompilerParams(vmem_limit_bytes=24 * 2**20),
        name="upward",
    )(*operands)


def operators(m2l_ops):
    count = m2l_ops.shape[0]
    return pl.pallas_call(
        operators_kernel,
        out_shape=jax.ShapeDtypeStruct((count // 2, RANK, 2 * RANK), BF16),
        in_specs=[whole(pltpu.HBM)],
        out_specs=whole(),
        scratch_shapes=[
            pltpu.VMEM((RANK, RANK, count), BF16),
            pltpu.VMEM((2, 16 * (count + 5), 128), F32),
            pltpu.SemaphoreType.DMA,
        ],
        compiler_params=pltpu.CompilerParams(vmem_limit_bytes=16 * 2**20),
        name="operators",
    )(pltpu.with_memory_space_constraint(jnp.transpose(m2l_ops, (1, 2, 0)), pltpu.HBM))


def far_field(table, own, below, above, m2l):
    held = (jnp.asarray(cross_section_picks()),)
    held = [pltpu.with_memory_space_constraint(x, pltpu.HBM) for x in held]
    return pl.pallas_call(
        far_kernel,
        out_shape=(
            jax.ShapeDtypeStruct((80, RANK), F32),
            jax.ShapeDtypeStruct((12, RANK, RANK), BF16),
        ),
        in_specs=[whole(pltpu.SMEM), whole(), whole(), whole(), whole()] + [whole(pltpu.HBM)],
        out_specs=(whole(),) * 2,
        scratch_shapes=[
            pltpu.VMEM((49 * 32, 128), BF16),
            pltpu.VMEM((49 * 32, 11 * 128), BF16),
            pltpu.SemaphoreType.DMA,
        ],
        compiler_params=pltpu.CompilerParams(vmem_limit_bytes=16 * 2**20),
        name="far_field",
    )(table, own, below, above, m2l, *held)


def top_levels(table, partial, device_ops, shared, root_ops):
    boxes, roots = pl.pallas_call(
        top_kernel,
        out_shape=(
            jax.ShapeDtypeStruct((RANK, BOX_DEV), F32),
            jax.ShapeDtypeStruct((NROOT, RANK), F32),
        ),
        in_specs=[whole(pltpu.SMEM)] + [whole()] * 3 + [whole(pltpu.HBM)],
        out_specs=(whole(), whole()),
        scratch_shapes=[
            pltpu.VMEM((96, 128), F32),
            pltpu.VMEM((96, 128), F32),
            pltpu.VMEM((128, 128), F32),
            pltpu.VMEM(root_ops.shape, BF16),
            pltpu.SemaphoreType.DMA,
        ],
        compiler_params=pltpu.CompilerParams(vmem_limit_bytes=16 * 2**20),
        name="top_levels",
    )(table, partial, device_ops, shared, pltpu.with_memory_space_constraint(root_ops, pltpu.HBM))
    return boxes.T, roots


def swapped(value, mask):
    devices = lax.axis_size(AXIS)
    return lax.ppermute(value, AXIS, [(s, s ^ mask) for s in range(devices)])


def swapped_columns(value):
    devices = lax.axis_size(AXIS)
    pairs = []
    for s in range(devices):
        column, place = divmod(s, 4)
        other = column + 1 if column % 2 == 1 else column - 1
        if 0 <= other < devices // 4:
            pairs.append((s, other * 4 + (place ^ 2)))
    return lax.ppermute(value, AXIS, pairs)


def body(offsets, forces, counts, uc2ue, m2m_ops, compress, m2l_ops, root_ops):
    me = lax.axis_index(AXIS)
    shared, block = upward(offsets, forces, counts, uc2ue, m2m_ops, compress)
    shared = lax.all_to_all(shared, AXIS, 0, 0, tiled=True)
    two = jnp.concatenate([block, swapped(block, 1)], axis=0)
    own = jnp.concatenate([two, swapped(two, 2)], axis=0)
    own, m2l = lax.optimization_barrier((own, operators(m2l_ops)))
    is_upper = me // 4 % 2 == 1
    low_side, high_side = own[:, :128], own[:, 128:]
    sibling = swapped(jnp.where(is_upper, low_side, high_side), 6)
    further = swapped_columns(jnp.where(is_upper, high_side, low_side))
    below = jnp.where(is_upper, sibling, further)
    above = jnp.where(is_upper, further, sibling)
    below = jnp.concatenate([below[64:], below[:64]], axis=0)
    above = jnp.concatenate([above[64:], above[:64]], axis=0)
    table = jnp.asarray(device_level_table())
    partial, device_ops = far_field(table, own, below, above, m2l)
    return top_levels(table, partial, device_ops, shared, root_ops)


def solution(mesh):
    placed = (P(None, AXIS), P(None, AXIS), P(AXIS), P(), P(), P(), P(), P())
    return jax.shard_map(
        body, mesh=mesh, in_specs=placed, out_specs=(P(AXIS, None), P()), check_vma=False
    )
```

```python
import functools

import jax
import jax.numpy as jnp
import ml_dtypes
import numpy as np
from jax import lax
from jax.experimental import pallas as pl
from jax.experimental.pallas import tpu as pltpu
from jax.sharding import PartitionSpec as P

SURF_ORDER = 6
NQ = 152
NCOEF = 456
RANK = 64
P_CAP = 128
LEAF_DEV = 64
BOX_DEV = 73
NROOT = 32
AXIS = "morton"
CHECK_RADIUS = 1.475
LEAF_UNROLL = 64

F32 = jnp.float32
BF16 = jnp.bfloat16


def surface_points():
    ticks = np.linspace(-1.0, 1.0, SURF_ORDER)
    last = SURF_ORDER - 1
    chosen = []
    for i in range(SURF_ORDER):
        for j in range(SURF_ORDER):
            for k in range(SURF_ORDER):
                if min(i, j, k) == 0 or max(i, j, k) == last:
                    chosen.append((ticks[i], ticks[j], ticks[k]))
    return CHECK_RADIUS * np.array(chosen).T


def direction_index():
    found = {}
    for u in range(-3, 4):
        for v in range(-3, 4):
            for w in range(-3, 4):
                if max(abs(u), abs(v), abs(w)) >= 2:
                    found[(u, v, w)] = len(found)
    return found


DIRS = direction_index()


def leaf_order():
    table = np.zeros((64, 64), np.float32)
    for leaf in range(64):
        x, y, z = leaf // 16, leaf // 4 % 4, leaf % 4
        octant = (x % 2) * 4 + (y % 2) * 2 + z % 2
        parent = (x // 2) * 4 + (y // 2) * 2 + z // 2
        table[leaf, octant * 8 + parent] = 1.0
    return table.astype(ml_dtypes.bfloat16)


def reachable(shift, target):
    return not (shift == -3 and target % 2 == 0) and not (shift == 3 and target % 2 == 1)


def cross_section_picks():
    table = np.zeros((4, 49 * 32, 128), np.float32)
    for place in range(4):
        y_bit, z_bit = place // 2, place % 2
        for pair in range(49):
            v, w = pair // 7 - 3, pair % 7 - 3
            for side, first, copies in ((4, 0, 1), (2, 16, 2)):
                for y in range(side):
                    for z in range(side):
                        if not (reachable(v, y) and reachable(w, z)):
                            continue
                        gy, gz = side * y_bit + y + v, side * z_bit + z + w
                        if not (0 <= gy < 2 * side and 0 <= gz < 2 * side):
                            continue
                        owner = (gy // side) * 2 + gz // side
                        source = (owner ^ place) * 32 + first + (gy % side) * side + gz % side
                        for copy in range(copies):
                            table[place, pair * 32 + first + 4 * copy + y * side + z, source] = 1.0
    return table.astype(ml_dtypes.bfloat16)


def device_level_table():
    rows = np.zeros((8, 24), np.int32)
    for place in range(8):
        parity, y_bit, z_bit = place // 4, place // 2 % 2, place % 2
        columns = (-2, 2, 3) if parity == 0 else (-2, -1, 3)
        for n, column in enumerate(columns):
            for other in range(4):
                entry = (column - parity, other // 2 - y_bit, other % 2 - z_bit)
                rows[place, n * 4 + other] = DIRS[entry]
            rows[place, 12 + n] = column
    return rows


def split(x):
    high = x.astype(BF16)
    return high, (x - high.astype(F32)).astype(BF16)


def stacked(x):
    high = x.astype(BF16).astype(F32)
    return jnp.concatenate([high, x - high], axis=0).astype(BF16)


def dot(a, b):
    return jnp.dot(a, b, preferred_element_type=F32)


def dot_nt(a, b):
    return lax.dot_general(a, b, (((1,), (1,)), ((), ())), preferred_element_type=F32)


def product(x, w_high, w_low, dot=dot):
    rows = x.shape[0]
    both = stacked(x)
    top = dot(both, w_high)
    rest = dot(both, w_low)
    return top[:rows] + (top[rows:] + rest[:rows])


def upward_kernel(
    offsets_hbm, forces_hbm, counts_hbm, surface_hbm, points_hbm, order_hbm, uc2ue_hbm, m2m_hbm,
    compress_hbm, shared, block,
    offsets, forces, counts, surface, points, order, uc2ue, m2m, compress,
    m2m_high, m2m_low, check, sems,
):
    pairs = (
        (offsets_hbm, offsets), (forces_hbm, forces), (counts_hbm, counts), (surface_hbm, surface),
        (points_hbm, points), (order_hbm, order), (uc2ue_hbm, uc2ue), (compress_hbm, compress),
        (m2m_hbm, m2m),
    )
    fetches = [pltpu.make_async_copy(a, b, sems.at[n]) for n, (a, b) in enumerate(pairs)]
    for fetch in fetches:
        fetch.start()
    for fetch in fetches[:4]:
        fetch.wait()
    slots = lax.broadcasted_iota(jnp.int32, (1, P_CAP), 1)
    zero = jnp.zeros((1, P_CAP), F32)
    one = jnp.ones((1, P_CAP), F32)

    def leaf(l, carry):
        columns = pl.ds(pl.multiple_of(l * P_CAP, P_CAP), P_CAP)
        u = offsets[:, columns]
        live = (slots < counts[l]).astype(F32)
        f = forces[:, columns] * live
        r = [surface[s] - u[s : s + 1] for s in range(3)]
        inverse = lax.rsqrt(r[0] * r[0] + r[1] * r[1] + r[2] * r[2])
        along = r[0] * f[0:1] + r[1] * f[1:2] + r[2] * f[2:3]
        pulled = along * (inverse * inverse * inverse)
        both = jnp.concatenate([inverse, pulled], axis=1)
        high, low = split(both)
        left = jnp.concatenate(
            [jnp.concatenate([f, zero], axis=0), jnp.concatenate([-u, one], axis=0)], axis=1
        )
        left = stacked(left)
        top = dot_nt(left, high)
        rest = dot_nt(left, low)
        sums = top[0:4] + (top[4:8] + rest[0:4])
        octant = (l >> 4 & 1) * 4 + (l >> 2 & 1) * 2 + (l & 1)
        parent = (l >> 5 & 1) * 4 + (l >> 3 & 1) * 2 + (l >> 1 & 1)
        check[pl.ds(octant * 8 + parent, 1)] = sums[None]
        return carry

    lax.fori_loop(0, LEAF_DEV, leaf, 0, unroll=LEAF_UNROLL)

    for fetch in fetches[4:8]:
        fetch.wait()
    density = jnp.zeros((LEAF_DEV, NCOEF), F32)
    for s in range(3):
        rows = check[:, s, :] + check[:, 3, :] * points[s : s + 1, :]
        w_high, w_low = split(uc2ue[s * NQ : (s + 1) * NQ, :])
        density = density + product(rows, w_high, w_low)
    shrink = compress[...]
    shrink = jnp.concatenate([shrink, shrink], axis=0)
    s_high, s_low = split(shrink)
    lower = lax.broadcasted_iota(jnp.int32, (1, 128), 1) < RANK
    leaves = product(density, s_high, s_low, dot_nt).astype(BF16)
    leaves = dot(order[...], leaves)
    block[0:16, 0:128] = jnp.where(lower, leaves[0:16], leaves[16:32]).astype(BF16)
    block[0:16, 128:256] = jnp.where(lower, leaves[32:48], leaves[48:64]).astype(BF16)

    fetches[8].wait()
    parents = jnp.zeros((8, NCOEF), F32)
    for o in range(8):
        w_high, w_low = split(m2m[o])
        m2m_high[o] = w_high
        m2m_low[o] = w_low
        parents = parents + product(density[o * 8 : o * 8 + 8], w_high, w_low)
    middle = product(parents, s_high, s_low, dot_nt).astype(BF16).astype(F32)
    middle = jnp.where(lower, middle[0:4], middle[4:8])

    def one_row(x, w_high, w_low, dot=dot):
        high, low = (part.astype(F32) for part in split(x))
        row = lax.broadcasted_iota(jnp.int32, (8, 1), 0)
        both = jnp.where(row == 0, high, jnp.where(row == 1, low, 0.0)).astype(BF16)
        top = dot(both, w_high)
        rest = dot(both, w_low)
        return top[0:1] + (top[1:2] + rest[0:1])

    device = jnp.zeros((1, NCOEF), F32)
    for o in range(8):
        device = device + one_row(parents[o : o + 1], m2m_high[o], m2m_low[o])
    own = one_row(device, s_high, s_low, dot_nt).astype(BF16).astype(F32)
    octant = lax.axis_index(AXIS) % 8
    above = one_row(device, m2m_high[octant], m2m_low[octant])
    above = one_row(above, s_high, s_low, dot_nt)
    shared[...] = jnp.broadcast_to(jnp.where(lower, own, above), shared.shape)
    middle = jnp.concatenate([middle, jnp.zeros((12, 128), F32)], axis=0).astype(BF16)
    block[16:32, 0:128] = middle
    block[16:32, 128:256] = middle


def operators_kernel(source_hbm, out, source, turned, sem):
    fetch = pltpu.make_async_copy(source_hbm, source, sem)
    fetch.start()
    directions = source.shape[2]
    rows = (directions + 7) // 8 * 8
    pitch = turned.shape[1] // 16
    shape = (rows, directions)
    unit = lax.broadcasted_iota(jnp.int32, shape, 0) == lax.broadcasted_iota(jnp.int32, shape, 1)
    unit = unit.astype(F32).astype(BF16)
    fetch.wait()
    for g in range(16):
        four = jnp.concatenate([source[g + 16 * part] for part in range(4)], axis=0)
        moved = dot_nt(unit, four)
        for half in range(2):
            turned[half, g * pitch : g * pitch + rows, :] = moved[:, half * 128 : half * 128 + 128]
    for d in range(directions):
        parts = []
        for half in range(2):
            pair = turned[half, pl.ds(d, 16, stride=pitch), :]
            parts += [pair, pltpu.roll(pair, RANK, 1)]
        out[d] = jnp.concatenate(parts, axis=0)[:, :RANK].astype(BF16)


def far_kernel(table, own, below, above, picks_hbm, m2l, boxes, device_ops, picks, near, sem):
    me = lax.axis_index(AXIS)
    fetch = pltpu.make_async_copy(picks_hbm.at[me % 4], picks, sem)
    fetch.start()
    lower = lax.broadcasted_iota(jnp.int32, (1, 128), 1) < RANK
    for n in range(12):
        device_ops[n] = m2l[table[me % 8, n]]

    x01, x23, x45, x67 = below[...], own[:, 0:128], own[:, 128:256], above[...]

    def crossed(a, b):
        return jnp.where(lower, pltpu.roll(a, RANK, 1), pltpu.roll(b, RANK, 1))

    x01, x23, x45, x67 = (x.astype(F32) for x in (x01, x23, x45, x67))
    none = jnp.zeros_like(x01)
    blocks = [
        x01, x23, x45, x67,
        crossed(x01, x23), crossed(x23, x45), crossed(x45, x67),
        crossed(none, x01), crossed(none, x23), crossed(x45, none), crossed(x67, none),
    ]
    wide = jnp.concatenate(blocks, axis=1).astype(BF16)
    fetch.wait()
    near[...] = dot(picks[...], wide).astype(BF16)

    def part(pair, rows, which):
        if which is None:
            return jnp.zeros((16, 128), BF16)
        first = pair * 32 + rows
        return near[first : first + 16, which * 128 : which * 128 + 128]

    even = {0: (7, 4, 5, 9), 1: (8, 5, 6, 10)}
    odd = {0: (0, 1, 2, None), 1: (1, 2, 3, None)}
    even_far = {0: (7, 2), 1: (8, 3)}
    odd_far = {0: (0, 9), 1: (1, 10)}
    level1 = ((7, 4, 6, 10), (0, 1, 3, None))
    level1_far = ((7, 3), (0, 10))
    first_rows = lax.broadcasted_iota(jnp.int32, (16, 128), 0) < 4
    total = jnp.zeros((80, RANK), F32)
    for pair in range(49):
        v, w = pair // 7 - 3, pair % 7 - 3
        close = max(abs(v), abs(w)) < 2
        shifts = (-3, -2, 2, 3) if close else range(-3, 4)
        e, o, l1 = (even_far, odd_far, level1_far) if close else (even, odd, level1)
        rows = []
        for halves in (e, o):
            for a in range(2):
                rows.append(jnp.concatenate([part(pair, 0, k) for k in halves[a]], axis=1))
        both = [
            jnp.where(first_rows, part(pair, 16, a).astype(F32), part(pair, 16, b).astype(F32)).astype(BF16)
            for a, b in zip(*l1)
        ]
        rows.append(jnp.concatenate(both, axis=1))
        left = jnp.concatenate(rows, axis=0)
        operator = [m2l[DIRS[(u, v, w)]] for u in shifts]
        if not close:
            left = left[:, : 7 * RANK]
        total = total + dot(left, jnp.concatenate(operator, axis=0))
    boxes[...] = jnp.zeros(boxes.shape, F32)
    boxes[1:9, :] = total[64:72]
    for p in range(2):
        for a in range(2):
            x = 2 * a + p
            first = (p * 2 + a) * 16
            boxes[9 + 16 * x : 25 + 16 * x, :] = total[first : first + 16]


def top_kernel(table, partial, device_ops, shared, root_ops, boxes, roots, base, shifted, turned):
    me = lax.axis_index(AXIS)
    lower = lax.broadcasted_iota(jnp.int32, (1, 128), 1) < RANK
    gathered = shared[...]
    high_half = jnp.sum(gathered.reshape(NROOT, 8, 128), axis=1).astype(BF16).astype(F32)
    low_half = pltpu.roll(high_half, RANK, 1)
    base[...] = jnp.zeros(base.shape, F32)
    shifted[...] = jnp.zeros(shifted.shape, F32)
    base[32:64, :] = jnp.where(lower, low_half, 0.0)
    shifted[31:63, :] = jnp.where(lower, 0.0, high_half)
    base[...] = base[...] + shifted[...]
    total = jnp.zeros((NROOT, RANK), F32)
    for distance in range(-31, 32, 2):
        if distance == -1:
            continue
        source = base[32 + distance : 64 + distance, :]
        first = distance + NROOT - 1
        if distance == 1:
            source = jnp.where(lower, 0.0, source)
        if distance == 31:
            total = total + dot(source[:, :RANK].astype(BF16), root_ops[first])
            continue
        operator = jnp.concatenate([root_ops[first], root_ops[first + 1]], axis=0)
        total = total + dot(source.astype(BF16), operator)
    roots[...] = total

    first_column = me // 8 * 2
    columns_total = lax.axis_size(AXIS) // 4
    far = jnp.zeros((8, RANK), F32)
    for n in range(3):
        column = first_column + table[me % 8, 12 + n]
        inside = jnp.logical_and(column >= 0, column < columns_total)
        kept = jnp.where(inside, 1.0, 0.0).astype(F32)
        start = jnp.clip(column, 0, columns_total - 1) * 4
        for other in range(4):
            source = shared[pl.ds(start + other, 1), :][:, :RANK] * kept
            source = jnp.broadcast_to(source, (8, RANK)).astype(BF16)
            far = far + dot(source, device_ops[n * 4 + other])
    turned[...] = jnp.zeros(turned.shape, F32)
    turned[0:80, 0:RANK] = partial[...]
    turned[0:1, 0:RANK] = far[0:1]
    boxes[...] = turned[...].T[:RANK, :BOX_DEV]


def whole(space=pltpu.VMEM):
    return pl.BlockSpec(memory_space=space)


def upward(offsets, forces, counts, uc2ue, m2m_ops, compress):
    devices = lax.axis_size(AXIS)
    points = surface_points().astype(np.float32)
    spread = np.ascontiguousarray(np.broadcast_to(points[:, :, None], (3, NQ, P_CAP)))
    rows = np.zeros((8, NQ), np.float32)
    rows[:3] = points
    operands = (
        offsets, forces, counts, jnp.asarray(spread), jnp.asarray(rows), jnp.asarray(leaf_order()),
        uc2ue, m2m_ops, compress.T,
    )
    operands = tuple(pltpu.with_memory_space_constraint(x, pltpu.HBM) for x in operands)
    held = [pltpu.VMEM(x.shape, x.dtype) for x in operands]
    held[2] = pltpu.SMEM(counts.shape, counts.dtype)
    return pl.pallas_call(
        upward_kernel,
        out_shape=(
            pltpu.VMEM((devices, 128), F32),
            pltpu.VMEM((32, 256), BF16),
        ),
        in_specs=[whole(pltpu.HBM)] * len(operands),
        out_specs=(whole(), whole()),
        scratch_shapes=held
        + [
            pltpu.VMEM((8, NCOEF, NCOEF), BF16),
            pltpu.VMEM((8, NCOEF, NCOEF), BF16),
            pltpu.VMEM((LEAF_DEV, 4, NQ), F32),
            pltpu.SemaphoreType.DMA((len(operands),)),
        ],
        compiler_params=pltpu.CompilerParams(vmem_limit_bytes=40 * 2**20),
        name="upward",
    )(*operands)


def operators(m2l_ops):
    count = m2l_ops.shape[0]
    return pl.pallas_call(
        operators_kernel,
        out_shape=jax.ShapeDtypeStruct(m2l_ops.shape, BF16),
        in_specs=[whole(pltpu.HBM)],
        out_specs=whole(),
        scratch_shapes=[
            pltpu.VMEM((RANK, RANK, count), BF16),
            pltpu.VMEM((2, 16 * (count + 5), 128), F32),
            pltpu.SemaphoreType.DMA,
        ],
        compiler_params=pltpu.CompilerParams(vmem_limit_bytes=28 * 2**20),
        name="operators",
    )(jnp.transpose(m2l_ops, (1, 2, 0)))


def far_field(table, own, below, above, m2l):
    return pl.pallas_call(
        far_kernel,
        out_shape=(
            jax.ShapeDtypeStruct((80, RANK), F32),
            jax.ShapeDtypeStruct((12, RANK, RANK), BF16),
        ),
        in_specs=[whole(pltpu.SMEM), whole(), whole(), whole(), whole(pltpu.HBM), whole()],
        out_specs=(whole(), whole()),
        scratch_shapes=[
            pltpu.VMEM((49 * 32, 128), BF16),
            pltpu.VMEM((49 * 32, 11 * 128), BF16),
            pltpu.SemaphoreType.DMA,
        ],
        compiler_params=pltpu.CompilerParams(vmem_limit_bytes=28 * 2**20),
        name="far_field",
    )(table, own, below, above, jnp.asarray(cross_section_picks()), m2l)


def top_levels(table, partial, device_ops, shared, root_ops):
    boxes, roots = pl.pallas_call(
        top_kernel,
        out_shape=(
            jax.ShapeDtypeStruct((RANK, BOX_DEV), F32),
            jax.ShapeDtypeStruct((NROOT, RANK), F32),
        ),
        in_specs=[whole(pltpu.SMEM)] + [whole()] * 4,
        out_specs=(whole(), whole()),
        scratch_shapes=[
            pltpu.VMEM((96, 128), F32),
            pltpu.VMEM((96, 128), F32),
            pltpu.VMEM((128, 128), F32),
        ],
        compiler_params=pltpu.CompilerParams(vmem_limit_bytes=16 * 2**20),
        name="top_levels",
    )(table, partial, device_ops, shared, root_ops)
    return boxes.T, roots


def swapped(value, mask):
    devices = lax.axis_size(AXIS)
    return lax.ppermute(value, AXIS, [(s, s ^ mask) for s in range(devices)])


def swapped_columns(value):
    devices = lax.axis_size(AXIS)
    pairs = []
    for s in range(devices):
        column, place = divmod(s, 4)
        other = column + 1 if column % 2 == 1 else column - 1
        if 0 <= other < devices // 4:
            pairs.append((s, other * 4 + (place ^ 2)))
    return lax.ppermute(value, AXIS, pairs)


def body(offsets, forces, counts, uc2ue, m2m_ops, compress, m2l_ops, root_ops):
    me = lax.axis_index(AXIS)
    shared, block = upward(offsets, forces, counts, uc2ue, m2m_ops, compress)
    shared = lax.all_to_all(shared, AXIS, 0, 0, tiled=True)
    two = jnp.concatenate([block, swapped(block, 1)], axis=0)
    own = jnp.concatenate([two, swapped(two, 2)], axis=0)
    is_upper = me // 4 % 2 == 1
    low_side, high_side = own[:, :128], own[:, 128:]
    sibling = swapped(jnp.where(is_upper, low_side, high_side), 6)
    further = swapped_columns(jnp.where(is_upper, high_side, low_side))
    below = jnp.where(is_upper, sibling, further)
    above = jnp.where(is_upper, further, sibling)
    below = jnp.concatenate([below[64:], below[:64]], axis=0)
    above = jnp.concatenate([above[64:], above[:64]], axis=0)
    table = jnp.asarray(device_level_table())
    partial, device_ops = far_field(table, own, below, above, operators(m2l_ops))
    return top_levels(table, partial, device_ops, shared, root_ops)


def solution(mesh):
    placed = (P(None, AXIS), P(None, AXIS), P(AXIS), P(), P(), P(), P(), P())
    return jax.shard_map(
        body, mesh=mesh, in_specs=placed, out_specs=(P(AXIS, None), P()), check_vma=False
    )
```
